32 devices in a mesh: tm: 2 (over y), mesh: 16 (over z, x, core).
Axes of the slice: x: 2, y: 2, z: 4, core: 2. Of those that a mesh axis runs over, the one named last changes fastest.
Arguments:
- inverse: bfloat16 [2, 135, 135, 2048], P('tm', None, None, 'mesh'), may hold values from -0.3 to 1.9
- start: float32 [2, 135, 2048], P('tm', None, 'mesh'), may hold values from -6 to 6
- source: float32 [2, 135, 2048], P('tm', None, 'mesh'), may hold values from -6 to 6
- mass: float32 [135, 2048], P(None, 'mesh'), may hold values from 0.1 to 1
- inner_elem: int32 [2, 4096], P(None, 'mesh'), may hold values from 0 to 127
- inner_face: int32 [2, 4096], P(None, 'mesh'), may hold values from 0 to 5
- inner_orient: int32 [4096], P('mesh'), may hold values from 0 to 7
- inner_jac: float32 [2, 2, 25, 4096], P('tm', None, None, 'mesh'), may hold values from -0.72 to 0.72
- cross_elem: int32 [16, 160], P('mesh'), may hold values from 0 to 127
- cross_face: int32 [16, 160], P('mesh'), may hold values from 0 to 5
- cross_orient: int32 [16, 160], P('mesh'), may hold values from 0 to 7, as said below
- cross_count: int32 [16, 5], P('mesh'), may hold values from 1 to 32, as said below
- cross_jac: float32 [2, 25, 16, 160], P('tm', None, 'mesh'), may hold values from -0.72 to 0.72
Outputs:
- adjoint: float32 [2, 135, 2048], P('tm', None, 'mesh')
The draws below stay inside these ranges and needn't reach their ends.
Inputs may be any that keep to these rules, and one draw needn't show every extreme that they name: cross_count[(p + off[k]) mod 16, mirror[k]] = cross_count[p, k], and cross_count[p, 3] = 32. cross_orient[(p + off[k]) mod 16, mirror[k] * 32 + s] = inv(cross_orient[p, k * 32 + s]).
All inputs are finite; a program needn't handle non-finite values.
Results may differ from the reference program's by a relative error of at most 0.008.
Values sent between devices are 32-bit elements; how exact they have to be, the bound alone decides.
A program may use at most 128 MiB of HBM per device.

```python
import math
import jax
import jax.numpy as jnp
import numpy as np
from jax import lax

BLK = 135
E_DEV = 128
FMAX = 32
SWEEPS = 2
FIN = 256
TIMES = 2
ELEMS = 2048
N_MESH = 16


def inverse_orientations():
    perm_table = np.zeros((8, 9), np.int32)
    for orient in range(8):
        for tangent_v in range(3):
            for tangent_u in range(3):
                moved_u, moved_v = (tangent_v, tangent_u) if orient // 4 else (tangent_u, tangent_v)
                if orient % 2:
                    moved_u = 2 - moved_u
                if orient // 2 % 2:
                    moved_v = 2 - moved_v
                perm_table[orient, 3 * tangent_v + tangent_u] = 3 * moved_v + moved_u
    inverse_table = np.zeros((8,), np.int32)
    for orient in range(8):
        for candidate in range(8):
            if np.all(perm_table[candidate][perm_table[orient]] == np.arange(9)):
                inverse_table[orient] = candidate
    return inverse_table


def draw_inverse(key, part):
    key = jax.random.fold_in(key, 11)
    noise_key, diag_key = jax.random.split(key)
    full_shape = (TIMES, BLK, BLK, ELEMS)
    noise = jnp.clip(jax.random.normal(noise_key, full_shape, jnp.float32), -6.0, 6.0)
    diagonal = jax.random.uniform(diag_key, (TIMES, BLK, 1, ELEMS), jnp.float32, 0.6, 1.4)
    identity = (jnp.arange(BLK)[:, None] == jnp.arange(BLK)[None, :]).astype(jnp.float32)
    return (noise * (0.5 / math.sqrt(BLK)) + identity[None, :, :, None] * diagonal).astype(jnp.bfloat16)


def draw_cross_orient(key, part):
    key = jax.random.fold_in(key, 12)
    raw_orient = jax.random.randint(key, (N_MESH, 5, FMAX), 0, 8, jnp.int32)
    inverse_row = jnp.asarray(inverse_orientations(), jnp.int32)
    half_way = N_MESH // 2
    first = raw_orient[:, 0]
    second = jnp.take(inverse_row, jnp.roll(first, 1, axis=0))
    third = raw_orient[:, 2]
    fifth = jnp.take(inverse_row, jnp.roll(third, half_way - 1, axis=0))
    rows_id = jnp.arange(N_MESH)[:, None]
    fourth = jnp.where(rows_id < half_way, raw_orient[:, 3], jnp.take(inverse_row, jnp.roll(raw_orient[:, 3], half_way, axis=0)))
    return jnp.stack([first, second, third, fourth, fifth], axis=1).reshape(N_MESH, 5 * FMAX).astype(jnp.int32)


def draw_cross_count(key, part):
    key = jax.random.fold_in(key, 13)
    raw_count = jax.random.randint(key, (N_MESH, 5), 1, FMAX + 1, jnp.int32)
    half_way = N_MESH // 2
    first = raw_count[:, 0]
    second = jnp.roll(first, 1)
    third = raw_count[:, 2]
    fifth = jnp.roll(third, half_way - 1)
    fourth = jnp.full((N_MESH,), FMAX, jnp.int32)
    return jnp.stack([first, second, third, fourth, fifth], axis=1).astype(jnp.int32)


def with_ends(result, key, smallest, largest):
    shape = result.shape
    spot = [jax.random.randint(jax.random.fold_in(key, axis), (), 0, shape[axis]) for axis in range(len(shape))]
    result = result.at[tuple(spot)].set(smallest)
    longest = shape.index(max(shape))
    spot[longest] = (spot[longest] + 1) % shape[longest]
    return result.at[tuple(spot)].set(largest)


def steps_of(key, extent, cuts, least, largest):
    def one(position, blocks):
        steps = jax.random.uniform(jax.random.fold_in(jax.random.fold_in(key, 6), position), (blocks,), jnp.float32, least / len(cuts), largest / len(cuts))
        return jnp.repeat(jnp.exp(steps), extent[position] // blocks).reshape((-1,) + (1,) * (len(extent) - position - 1))

    level = one(*cuts[0])
    for cut in cuts[1:]:
        level = level * one(*cut)
    return level


def bell_draw(stream_key, shape, spread, most, shards=(), kind=jnp.bfloat16):
    entries = jax.random.normal(stream_key, shape, jnp.float32) * spread
    if len(shards) > 0:
        entries = steps_of(stream_key, shape, shards, -0.22, 0.18) * entries
    return jnp.clip(entries, min=-most, max=most).astype(kind)


def setup_inputs(seed: int = 0) -> dict:
    key_of = jax.random.split(jax.random.key(seed), 14)
    return {
        "inverse": draw_inverse(jax.random.fold_in(key_of[13], 71), 0),
        "start": bell_draw(key_of[1], (TIMES, BLK, ELEMS), 1.0, 6.0, ((0, 2), (2, 16)), jnp.float32),
        "source": bell_draw(key_of[2], (TIMES, BLK, ELEMS), 1.0, 6.0, ((0, 2), (2, 16)), jnp.float32),
        "mass": jnp.clip(jnp.exp(math.log(1.0) - 2.3025851 * jax.random.uniform(key_of[3], (BLK, ELEMS), jnp.float32) ** steps_of(key_of[3], (BLK, ELEMS), ((1, 16),), -0.2, 0.2)), 0.1, 1.0),
        "inner_elem": with_ends(jax.random.randint(key_of[4], (2, N_MESH * FIN), 0, E_DEV), jax.random.fold_in(key_of[4], 1), 0, E_DEV - 1).astype(jnp.int32),
        "inner_face": with_ends(jax.random.randint(key_of[5], (2, N_MESH * FIN), 0, 6), jax.random.fold_in(key_of[5], 1), 0, 5).astype(jnp.int32),
        "inner_orient": with_ends(jax.random.randint(key_of[6], (N_MESH * FIN,), 0, 8), jax.random.fold_in(key_of[6], 1), 0, 7).astype(jnp.int32),
        "inner_jac": bell_draw(key_of[7], (TIMES, 2, 25, N_MESH * FIN), 0.12, 0.72, ((0, 2), (3, 16)), jnp.float32),
        "cross_elem": with_ends(jax.random.randint(key_of[8], (N_MESH, 5 * FMAX), 0, E_DEV), jax.random.fold_in(key_of[8], 1), 0, E_DEV - 1).astype(jnp.int32),
        "cross_face": with_ends(jax.random.randint(key_of[9], (N_MESH, 5 * FMAX), 0, 6), jax.random.fold_in(key_of[9], 1), 0, 5).astype(jnp.int32),
        "cross_orient": draw_cross_orient(jax.random.fold_in(key_of[13], 71), 0),
        "cross_count": draw_cross_count(jax.random.fold_in(key_of[13], 71), 0),
        "cross_jac": bell_draw(key_of[12], (TIMES, 25, N_MESH, 5 * FMAX), 0.12, 0.72, ((0, 2), (2, 16)), jnp.float32),
    }


line_weights = (1.0 / 3.0, 4.0 / 3.0, 1.0 / 3.0)
highest = lax.Precision.HIGHEST
mirror_list = (1, 0, 4, 3, 2)


def build_tables():
    face_nodes = np.zeros((6, 9), np.int32)
    face_weight = np.zeros((9,), np.float32)
    for face_index in range(6):
        normal_axis = face_index // 2
        tangent_axes = [other_axis for other_axis in range(3) if other_axis != normal_axis]
        for tangent_v in range(3):
            for tangent_u in range(3):
                coords = [0, 0, 0]
                coords[normal_axis] = 2 * (face_index % 2)
                coords[tangent_axes[0]] = tangent_u
                coords[tangent_axes[1]] = tangent_v
                face_nodes[face_index, 3 * tangent_v + tangent_u] = 9 * coords[2] + 3 * coords[1] + coords[0]
                face_weight[3 * tangent_v + tangent_u] = line_weights[tangent_u] * line_weights[tangent_v]
    perm_table = np.zeros((8, 9), np.int32)
    for orient in range(8):
        for tangent_v in range(3):
            for tangent_u in range(3):
                moved_u, moved_v = (tangent_v, tangent_u) if orient // 4 else (tangent_u, tangent_v)
                if orient % 2:
                    moved_u = 2 - moved_u
                if (orient // 2) % 2:
                    moved_v = 2 - moved_v
                perm_table[orient, 3 * tangent_v + tangent_u] = 3 * moved_v + moved_u
    inverse_table = np.zeros((8,), np.int32)
    for orient in range(8):
        for candidate in range(8):
            if np.all(perm_table[candidate][perm_table[orient]] == np.arange(9)):
                inverse_table[orient] = candidate
    return face_nodes, face_weight, perm_table, inverse_table


def time_matrix(count_times):
    table = [0.0] * count_times
    for offset in range(1, count_times):
        parity = (-1.0) ** offset
        phase = math.pi * offset / count_times
        table[offset] = 0.3 * parity * math.cos(phase) / math.sin(phase) + 1.2 * parity / count_times
    matrix = [[table[(col_index - row_index) % count_times] for col_index in range(count_times)] for row_index in range(count_times)]
    return np.array(matrix, np.float32)


def couple(state, jacobian, send_col, send_face, recv_col, recv_face, orients, live):
    face_nodes, face_weight, perm_table, inverse_table = build_tables()
    node_table = jnp.asarray(face_nodes)
    slot_total = send_col.shape[0]
    gathered = state[:, send_col].reshape(5, 27, slot_total)
    send_nodes = node_table[send_face].T
    trace = jnp.take_along_axis(gathered, send_nodes[None], axis=1) * jnp.asarray(face_weight)[None, :, None]
    perm_rows = jnp.asarray(perm_table)[orients].T
    permuted = jnp.take_along_axis(trace, perm_rows[None], axis=1)
    received = jnp.einsum('uvs,uns->vns', jacobian.reshape(5, 5, slot_total), permuted, precision=highest)
    received = jnp.where(live[None, None, :], received, 0.0)
    recv_nodes = node_table[recv_face].T
    total = jnp.zeros((5, 27, state.shape[1]), jnp.float32)
    total = total.at[:, recv_nodes, recv_col[None, :]].add(received)
    return total.reshape(BLK, state.shape[1])


def reference(inverse, start, source, mass, inner_elem, inner_face, inner_orient, inner_jac, cross_elem, cross_face, cross_orient, cross_count, cross_jac):
    face_nodes, face_weight, perm_table, inverse_table = build_tables()
    parts = N_MESH
    inner_base = (jnp.arange(parts * FIN, dtype=jnp.int32) // FIN) * E_DEV
    column_a = inner_base + inner_elem[0]
    column_b = inner_base + inner_elem[1]
    back_orient = jnp.asarray(inverse_table)[inner_orient].astype(jnp.int32)
    offsets = jnp.asarray([1, parts - 1, parts // 2 - 1, parts // 2, parts // 2 + 1], jnp.int32)
    mirror = jnp.asarray(mirror_list, jnp.int32)
    cube_elem = cross_elem.reshape(parts, 5, FMAX)
    cube_face = cross_face.reshape(parts, 5, FMAX)
    part_index = jnp.arange(parts, dtype=jnp.int32)
    partner = ((part_index[:, None] + offsets[None, :]) % parts).astype(jnp.int32)
    mirror_grid = jnp.broadcast_to(mirror[None, :], (parts, 5))
    send_elem = cube_elem[partner, mirror_grid]
    send_face_cube = cube_face[partner, mirror_grid]
    recv_cross = (part_index[:, None, None] * E_DEV + cube_elem).reshape(-1)
    send_cross = (partner[:, :, None] * E_DEV + send_elem).reshape(-1)
    slot_index = jnp.arange(FMAX, dtype=jnp.int32)
    live_cross = (slot_index[None, None, :] < cross_count[:, :, None]).reshape(-1)
    send_col = jnp.concatenate([column_b, column_a, send_cross]).astype(jnp.int32)
    send_face = jnp.concatenate([inner_face[1], inner_face[0], send_face_cube.reshape(-1)]).astype(jnp.int32)
    recv_col = jnp.concatenate([column_a, column_b, recv_cross]).astype(jnp.int32)
    recv_face = jnp.concatenate([inner_face[0], inner_face[1], cross_face.reshape(-1)]).astype(jnp.int32)
    orients = jnp.concatenate([inner_orient, back_orient, cross_orient.reshape(-1)]).astype(jnp.int32)
    live = jnp.concatenate([jnp.ones((2 * parts * FIN,), bool), live_cross])
    jac_all = jnp.concatenate([inner_jac[:, 0], inner_jac[:, 1], cross_jac.reshape(TIMES, 25, -1)], axis=2)
    matrix = jnp.asarray(time_matrix(TIMES))
    current = start
    for sweep_index in range(SWEEPS):
        coupling = lax.map(lambda operands: couple(operands[0], operands[1], send_col, send_face, recv_col, recv_face, orients, live), (current, jac_all))
        spectral = jnp.einsum('ts,sie->tie', matrix, current, precision=highest)
        resid = (source - coupling - mass[None] * spectral).astype(jnp.bfloat16)
        current = lax.map(lambda operands: jnp.einsum('ije,je->ie', operands[0].astype(jnp.float32), operands[1].astype(jnp.float32), precision=highest), (inverse, resid))
    return current
```

```python
import functools
import math

import jax
import jax.numpy as jnp
import numpy as np
from jax import lax
from jax.experimental import pallas as pl
from jax.experimental.pallas import tpu as pltpu
from jax.sharding import PartitionSpec as P

SWEEPS = 2
VARS = 5
NODES = 27
MIRROR = (1, 0, 4, 3, 2)
LINE_WEIGHTS = (1.0 / 3.0, 4.0 / 3.0, 1.0 / 3.0)
MESH = pl.DeviceIdType.MESH


def face_table():
    nodes = [[0] * 9 for _ in range(6)]
    weight = [1.0] * NODES
    for face in range(6):
        normal = face // 2
        tangent = [axis for axis in range(3) if axis != normal]
        for j in range(3):
            for i in range(3):
                coords = [0, 0, 0]
                coords[normal] = 2 * (face % 2)
                coords[tangent[0]] = i
                coords[tangent[1]] = j
                node = 9 * coords[2] + 3 * coords[1] + coords[0]
                nodes[face][3 * j + i] = node
                weight[node] = float(np.float32(LINE_WEIGHTS[i] * LINE_WEIGHTS[j]))
    return nodes, weight


FACE_NODES, NODE_WEIGHT = face_table()


def coef_table(count):
    table = [0.0] * count
    for k in range(1, count):
        parity = (-1.0) ** k
        phase = math.pi * k / count
        table[k] = 0.3 * parity * math.cos(phase) / math.sin(phase) + 1.2 * parity / count
    return [float(np.float32(c)) for c in table]


def split_rows(value):
    high = value.astype(jnp.bfloat16).astype(jnp.float32)
    return jnp.concatenate([high, value - high], axis=0).astype(jnp.bfloat16)


def orient_back(orient):
    swapped = 4 + 2 * (orient & 1) + ((orient >> 1) & 1)
    return jnp.where(orient >= 4, swapped, orient)


def apply_orient(trace, orient):
    shape = trace[0].shape
    flip_i = jnp.broadcast_to((orient & 1) == 1, shape)
    flip_j = jnp.broadcast_to((orient & 2) == 2, shape)
    swap = jnp.broadcast_to(orient >= 4, shape)
    step = [
        trace[3 * j + i] if i == 1 else jnp.where(flip_i, trace[3 * j + 2 - i], trace[3 * j + i])
        for j in range(3)
        for i in range(3)
    ]
    step = [
        step[3 * j + i] if j == 1 else jnp.where(flip_j, step[3 * (2 - j) + i], step[3 * j + i])
        for j in range(3)
        for i in range(3)
    ]
    return [
        step[3 * j + i] if i == j else jnp.where(swap, step[3 * i + j], step[3 * j + i])
        for j in range(3)
        for i in range(3)
    ]


def apply_jacobian(jac, trace):
    received = []
    for value in trace:
        total = jac[0] * value[0:1, :]
        for u in range(1, VARS):
            total = total + jac[u] * value[u : u + 1, :]
        received.append(total)
    return received


def kernel(
    count_times,
    count_mesh,
    inverse,
    start,
    source,
    mass,
    inner_elem,
    inner_face,
    inner_orient,
    inner_jac,
    cross_elem,
    cross_face,
    cross_orient,
    cross_count,
    cross_jac,
    out,
    inv_v,
    hot_inner,
    hot_cross,
    state,
    jac,
    couple,
    resid,
    current,
    send_buf,
    recv_buf,
    peer_buf,
    inv_sem,
    send_sem,
    recv_sem,
    peer_send_sem,
    peer_recv_sem,
):
    elems = start.shape[1]
    fin = inner_orient.shape[1]
    slots = cross_orient.shape[1]
    cap = slots // 5
    lanes = hot_cross.shape[1]
    chunk = inv_v.shape[0] // 5
    me = lax.axis_index("mesh")
    mine = lax.axis_index("tm")
    offsets = [1, count_mesh - 1, count_mesh // 2 - 1, count_mesh // 2, count_mesh // 2 + 1]
    partners = [lax.rem(me + off, count_mesh) for off in offsets]
    peers = [lax.rem(mine - d + count_times, count_times) for d in range(1, count_times)]
    coef = coef_table(count_times)

    loads = [
        pltpu.make_async_copy(
            inverse.at[pl.ds(c * chunk, chunk)], inv_v.at[pl.ds(c * chunk, chunk)], inv_sem.at[c]
        )
        for c in range(5)
    ]
    for load in loads:
        load.start()

    barrier = pltpu.get_barrier_semaphore()
    for partner in partners:
        pl.semaphore_signal(barrier, inc=1, device_id={"mesh": partner}, device_id_type=MESH)
    for peer in peers:
        pl.semaphore_signal(barrier, inc=1, device_id={"tm": peer}, device_id_type=MESH)

    cross_key = cross_face[...] * elems + cross_elem[...]
    cross_key = jnp.concatenate(
        [cross_key, jnp.full((1, lanes - slots), -1, jnp.int32)], axis=1
    )
    inner_key = inner_face[...] * elems + inner_elem[...]
    inner_key = jnp.concatenate([inner_key[0:1], inner_key[1:2]], axis=1)
    for face in range(6):
        rows = lax.broadcasted_iota(jnp.int32, (elems, lanes), 0) + face * elems
        hot_cross[pl.ds(face * elems, elems), :] = jnp.where(
            rows == cross_key, 1.0, 0.0
        ).astype(jnp.bfloat16)
        rows = lax.broadcasted_iota(jnp.int32, (elems, 2 * fin), 0) + face * elems
        hot_inner[pl.ds(face * elems, elems), :] = jnp.where(
            rows == inner_key, 1.0, 0.0
        ).astype(jnp.bfloat16)

    jac[...] = jnp.zeros_like(jac)
    for u in range(VARS):
        for v in range(VARS):
            jac[u, v : v + 1, 0:fin] = inner_jac[5 * u + v, 0:1, :]
            jac[u, v : v + 1, fin : 2 * fin] = inner_jac[5 * u + v, 1:2, :]
            jac[u, v : v + 1, 2 * fin : 2 * fin + slots] = cross_jac[5 * u + v, :, :]

    orient = inner_orient[...]
    inner_orients = jnp.concatenate([orient, orient_back(orient)], axis=1)
    cross_orients = jnp.concatenate(
        [cross_orient[...], jnp.zeros((1, lanes - slots), jnp.int32)], axis=1
    )
    lane = lax.broadcasted_iota(jnp.int32, (1, lanes), 1)
    live = jnp.zeros((1, lanes), jnp.int32)
    for k in range(5):
        live = jnp.where((lane >= k * cap) & (lane < k * cap + cross_count[0, k]), 1, live)
    live = jnp.broadcast_to(live == 1, (8, lanes))
    group = lax.broadcasted_iota(jnp.int32, (8, 128), 1) // cap

    state[...] = jnp.zeros_like(state)
    resid[...] = jnp.zeros_like(resid)
    zero_tile = jnp.zeros((8, 128), jnp.float32)

    for sweep in range(SWEEPS):
        now = start if sweep == 0 else current
        for v in range(VARS):
            state[pl.ds(v, NODES, stride=8), :] = now[v * NODES : (v + 1) * NODES, :]
        peer_copies = [
            pltpu.make_async_remote_copy(
                src_ref=now,
                dst_ref=peer_buf.at[sweep, d],
                send_sem=peer_send_sem.at[sweep, d],
                recv_sem=peer_recv_sem.at[sweep, d],
                device_id={"tm": peers[d]},
                device_id_type=MESH,
            )
            for d in range(count_times - 1)
        ]
        if sweep > 0:
            for copy in peer_copies:
                copy.start()
        tiles = [
            state[8 * node : 8 * node + 8, :] * NODE_WEIGHT[node] for node in range(NODES)
        ]
        faces = jnp.concatenate(
            [
                jnp.concatenate([tiles[FACE_NODES[face][n]] for face in range(6)], axis=1)
                for n in range(9)
            ],
            axis=0,
        )
        faces = split_rows(faces)

        cross_trace = jnp.dot(faces, hot_cross[...], preferred_element_type=jnp.float32)
        cross_trace = cross_trace[0:72] + cross_trace[72:144]
        for k in range(5):
            column = (k // 4) * 128
            for h in range(3):
                packed = zero_tile
                for g in range(4):
                    n = 4 * h + g
                    if n < 9:
                        piece = cross_trace[8 * n : 8 * n + 8, column : column + 128]
                        shift = (g - k % 4) * cap % 128
                        piece = pltpu.roll(piece, shift, 1) if shift else piece
                        packed = jnp.where(group == g, piece, packed)
                send_buf[sweep, k, 8 * h : 8 * h + 8, :] = packed
        if sweep == 0:
            pl.semaphore_wait(barrier, 5 + count_times - 1)
        copies = [
            pltpu.make_async_remote_copy(
                src_ref=send_buf.at[sweep, k],
                dst_ref=recv_buf.at[sweep, MIRROR[k]],
                send_sem=send_sem.at[sweep, k],
                recv_sem=recv_sem.at[sweep, MIRROR[k]],
                device_id={"mesh": partners[k]},
                device_id_type=MESH,
            )
            for k in range(5)
        ]
        for k in (3, 2, 4, 0, 1):
            copies[k].start()
        if sweep == 0:
            for copy in peer_copies:
                copy.start()

        trace = jnp.dot(faces, hot_inner[...], preferred_element_type=jnp.float32)
        trace = trace[0:72] + trace[72:144]
        trace = [
            jnp.concatenate(
                [trace[8 * n : 8 * n + 8, fin:], trace[8 * n : 8 * n + 8, :fin]], axis=1
            )
            for n in range(9)
        ]
        trace = apply_orient(trace, inner_orients)
        received = apply_jacobian([jac[u, :, 0 : 2 * fin] for u in range(VARS)], trace)
        received = split_rows(jnp.concatenate(received, axis=0))
        placed = lax.dot_general(
            received,
            hot_inner[...],
            (((1,), (1,)), ((), ())),
            preferred_element_type=jnp.float32,
        )
        inner_placed = placed[0:72] + placed[72:144]

        for copy in copies:
            copy.wait_recv()
        arrived = []
        for n in range(9):
            h, g = n // 4, n % 4
            columns = [zero_tile] * (lanes // 128)
            for k in range(5):
                piece = recv_buf[sweep, k, 8 * h : 8 * h + 8, :]
                shift = (k % 4 - g) * cap % 128
                piece = pltpu.roll(piece, shift, 1) if shift else piece
                columns[k // 4] = jnp.where(group == k % 4, piece, columns[k // 4])
            arrived.append(jnp.concatenate(columns, axis=1))
        arrived = apply_orient(arrived, cross_orients)
        received = apply_jacobian([jac[u, :, 2 * fin :] for u in range(VARS)], arrived)
        received = [jnp.where(live, value, 0.0) for value in received]
        received = split_rows(jnp.concatenate(received, axis=0))
        placed = lax.dot_general(
            received,
            hot_cross[...],
            (((1,), (1,)), ((), ())),
            preferred_element_type=jnp.float32,
        )
        placed = placed[0:72] + placed[72:144] + inner_placed

        totals = [zero_tile] * NODES
        for face in range(6):
            for n in range(9):
                node = FACE_NODES[face][n]
                totals[node] = (
                    totals[node] + placed[8 * n : 8 * n + 8, face * elems : (face + 1) * elems]
                )
        for node in range(NODES):
            couple[8 * node : 8 * node + 8, :] = totals[node]

        for copy in peer_copies:
            copy.wait_recv()
        for v in range(VARS):
            rows = slice(v * NODES, (v + 1) * NODES)
            spectral = coef[1] * peer_buf[sweep, 0, rows, :]
            for d in range(1, count_times - 1):
                spectral = spectral + coef[d + 1] * peer_buf[sweep, d, rows, :]
            value = (
                source[rows, :]
                - couple[pl.ds(v, NODES, stride=8), :]
                - mass[rows, :] * spectral
            )
            resid[rows, :] = value.astype(jnp.bfloat16).astype(jnp.float32)

        for copy in peer_copies:
            copy.wait_send()
        for copy in copies:
            copy.wait_send()
        if sweep == 0:
            for load in loads:
                load.wait()
        target = out if sweep == SWEEPS - 1 else current
        top = resid[0:128, :].reshape(16, 8, 128)
        tail = resid[128:136, :]

        def row_sum(row):
            block = inv_v[row, 0:128, :].astype(jnp.float32).reshape(16, 8, 128)
            last = inv_v[row, 128:135, :].astype(jnp.float32)
            last = jnp.concatenate([last, jnp.zeros((1, 128), jnp.float32)], axis=0)
            total = jnp.sum(block * top, axis=0) + last * tail
            return jnp.sum(total, axis=0, keepdims=True)

        def body(step, carry):
            base = pl.multiple_of(step * 8, 8)
            sums = [row_sum(base + i) for i in range(8)]
            target[pl.ds(base, 8), :] = jnp.concatenate(sums, axis=0)
            return carry

        lax.fori_loop(0, 16, body, 0)
        sums = [row_sum(128 + i) for i in range(7)]
        target[128:135, :] = jnp.concatenate(sums, axis=0)


def on_device(
    inverse,
    start,
    source,
    mass,
    inner_elem,
    inner_face,
    inner_orient,
    inner_jac,
    cross_elem,
    cross_face,
    cross_orient,
    cross_count,
    cross_jac,
):
    count_times = lax.axis_size("tm")
    count_mesh = lax.axis_size("mesh")
    rows, elems = mass.shape
    fin = inner_orient.shape[0]
    slots = cross_elem.shape[1]
    lanes = -(-slots // 128) * 128
    vmem = pl.BlockSpec(memory_space=pltpu.VMEM)
    specs = [vmem] * 13
    specs[0] = pl.BlockSpec(memory_space=pl.ANY)
    specs[11] = pl.BlockSpec(memory_space=pltpu.SMEM)
    result = pl.pallas_call(
        functools.partial(kernel, count_times, count_mesh),
        out_shape=jax.ShapeDtypeStruct((rows, elems), jnp.float32),
        in_specs=specs,
        out_specs=vmem,
        scratch_shapes=[
            pltpu.VMEM((rows, rows, elems), jnp.bfloat16),
            pltpu.VMEM((6 * elems, 2 * fin), jnp.bfloat16),
            pltpu.VMEM((6 * elems, lanes), jnp.bfloat16),
            pltpu.VMEM((8 * NODES, elems), jnp.float32),
            pltpu.VMEM((VARS, 8, 2 * fin + lanes), jnp.float32),
            pltpu.VMEM((8 * NODES, elems), jnp.float32),
            pltpu.VMEM((136, elems), jnp.float32),
            pltpu.VMEM((rows, elems), jnp.float32),
            pltpu.VMEM((SWEEPS, 5, 24, 128), jnp.float32),
            pltpu.VMEM((SWEEPS, 5, 24, 128), jnp.float32),
            pltpu.VMEM((SWEEPS, count_times - 1, rows, elems), jnp.float32),
            pltpu.SemaphoreType.DMA((5,)),
            pltpu.SemaphoreType.DMA((SWEEPS, 5)),
            pltpu.SemaphoreType.DMA((SWEEPS, 5)),
            pltpu.SemaphoreType.DMA((SWEEPS, count_times - 1)),
            pltpu.SemaphoreType.DMA((SWEEPS, count_times - 1)),
        ],
        compiler_params=pltpu.CompilerParams(
            collective_id=0, has_side_effects=True, vmem_limit_bytes=40 * 1024 * 1024
        ),
    )(
        inverse[0],
        start[0],
        source[0],
        mass,
        inner_elem,
        inner_face,
        inner_orient.reshape(1, fin),
        jnp.transpose(inner_jac[0], (1, 0, 2)),
        cross_elem,
        cross_face,
        cross_orient,
        cross_count,
        cross_jac[0],
    )
    return result[None]


def solution(mesh):
    in_specs = (
        P("tm", None, None, "mesh"),
        P("tm", None, "mesh"),
        P("tm", None, "mesh"),
        P(None, "mesh"),
        P(None, "mesh"),
        P(None, "mesh"),
        P("mesh"),
        P("tm", None, None, "mesh"),
        P("mesh", None),
        P("mesh", None),
        P("mesh", None),
        P("mesh", None),
        P("tm", None, "mesh", None),
    )
    out_specs = P("tm", None, "mesh")
    return jax.shard_map(
        on_device, mesh=mesh, in_specs=in_specs, out_specs=out_specs, check_vma=False
    )
```

```python
import functools
import math

import jax
import jax.numpy as jnp
import numpy as np
from jax import lax
from jax.experimental import pallas as pl
from jax.experimental.pallas import tpu as pltpu
from jax.sharding import PartitionSpec as P

SWEEPS = 2
VARS = 5
NODES = 27
MIRROR = (1, 0, 4, 3, 2)
LINE_WEIGHTS = (1.0 / 3.0, 4.0 / 3.0, 1.0 / 3.0)
MESH = pl.DeviceIdType.MESH


def face_table():
    nodes = [[0] * 9 for _ in range(6)]
    weight = [1.0] * NODES
    for face in range(6):
        normal = face // 2
        tangent = [axis for axis in range(3) if axis != normal]
        for j in range(3):
            for i in range(3):
                coords = [0, 0, 0]
                coords[normal] = 2 * (face % 2)
                coords[tangent[0]] = i
                coords[tangent[1]] = j
                node = 9 * coords[2] + 3 * coords[1] + coords[0]
                nodes[face][3 * j + i] = node
                weight[node] = float(np.float32(LINE_WEIGHTS[i] * LINE_WEIGHTS[j]))
    return nodes, weight


FACE_NODES, NODE_WEIGHT = face_table()


def coef_table(count):
    table = [0.0] * count
    for k in range(1, count):
        parity = (-1.0) ** k
        phase = math.pi * k / count
        table[k] = 0.3 * parity * math.cos(phase) / math.sin(phase) + 1.2 * parity / count
    return [float(np.float32(c)) for c in table]


def split_rows(value):
    high = value.astype(jnp.bfloat16).astype(jnp.float32)
    return jnp.concatenate([high, value - high], axis=0).astype(jnp.bfloat16)


def orient_back(orient):
    swapped = 4 + 2 * (orient & 1) + ((orient >> 1) & 1)
    return jnp.where(orient >= 4, swapped, orient)


def apply_orient(trace, orient):
    shape = trace[0].shape
    flip_i = jnp.broadcast_to((orient & 1) == 1, shape)
    flip_j = jnp.broadcast_to((orient & 2) == 2, shape)
    swap = jnp.broadcast_to(orient >= 4, shape)
    step = [
        trace[3 * j + i] if i == 1 else jnp.where(flip_i, trace[3 * j + 2 - i], trace[3 * j + i])
        for j in range(3)
        for i in range(3)
    ]
    step = [
        step[3 * j + i] if j == 1 else jnp.where(flip_j, step[3 * (2 - j) + i], step[3 * j + i])
        for j in range(3)
        for i in range(3)
    ]
    return [
        step[3 * j + i] if i == j else jnp.where(swap, step[3 * i + j], step[3 * j + i])
        for j in range(3)
        for i in range(3)
    ]


def apply_jacobian(jac, trace):
    received = []
    for value in trace:
        total = jac[0] * value[0:1, :]
        for u in range(1, VARS):
            total = total + jac[u] * value[u : u + 1, :]
        received.append(total)
    return received


def kernel(
    count_times,
    count_mesh,
    inverse,
    start_h,
    source_h,
    mass_h,
    inner_elem_h,
    inner_face_h,
    inner_orient_h,
    inner_jac_h,
    cross_elem_h,
    cross_face_h,
    cross_orient_h,
    cross_count_h,
    cross_jac_h,
    out,
    source,
    mass,
    inner_elem,
    inner_face,
    inner_orient,
    inner_jac,
    cross_elem,
    cross_face,
    cross_orient,
    cross_count,
    cross_jac,
    inv_v,
    hot_inner,
    hot_cross,
    state,
    jac,
    couple,
    resid,
    current,
    send_buf,
    recv_buf,
    peer_buf,
    load_sem,
    inv_sem,
    send_sem,
    recv_sem,
    peer_send_sem,
    peer_recv_sem,
):
    elems = mass.shape[1]
    fin = inner_orient.shape[1]
    slots = cross_orient.shape[1]
    cap = slots // 5
    lanes = hot_cross.shape[1]
    chunk = inv_v.shape[0] // 5
    me = lax.axis_index("mesh")
    mine = lax.axis_index("tm")
    offsets = [1, count_mesh - 1, count_mesh // 2 - 1, count_mesh // 2, count_mesh // 2 + 1]
    partners = [lax.rem(me + off, count_mesh) for off in offsets]
    peers = [lax.rem(mine - d + count_times, count_times) for d in range(1, count_times)]
    coef = coef_table(count_times)

    loads = [
        pltpu.make_async_copy(
            inverse.at[pl.ds(c * chunk, chunk)], inv_v.at[pl.ds(c * chunk, chunk)], inv_sem.at[c]
        )
        for c in range(5)
    ]
    pairs = {
        "cross_face": (cross_face_h, cross_face),
        "cross_elem": (cross_elem_h, cross_elem),
        "start": (start_h.at[:, 0], current),
        "inner_face": (inner_face_h, inner_face),
        "inner_elem": (inner_elem_h, inner_elem),
        "inner_orient": (inner_orient_h, inner_orient),
        "inner_jac": (inner_jac_h, inner_jac),
        "cross_orient": (cross_orient_h, cross_orient),
        "cross_count": (cross_count_h, cross_count),
        "cross_jac": (cross_jac_h, cross_jac),
        "source": (source_h.at[:, 0], source),
        "mass": (mass_h, mass),
    }
    arrays = {
        name: pltpu.make_async_copy(src, dst, load_sem.at[index])
        for index, (name, (src, dst)) in enumerate(pairs.items())
    }
    for load in arrays.values():
        load.start()
    for load in loads:
        load.start()

    barrier = pltpu.get_barrier_semaphore()
    for partner in partners:
        pl.semaphore_signal(barrier, inc=1, device_id={"mesh": partner}, device_id_type=MESH)
    for peer in peers:
        pl.semaphore_signal(barrier, inc=1, device_id={"tm": peer}, device_id_type=MESH)

    state[...] = jnp.zeros_like(state)
    resid[...] = jnp.zeros_like(resid)
    jac[...] = jnp.zeros_like(jac)
    zero_tile = jnp.zeros((8, 128), jnp.float32)
    group = lax.broadcasted_iota(jnp.int32, (8, 128), 1) // cap
    row = lax.broadcasted_iota(jnp.int32, (8, 128), 0)

    arrays["cross_face"].wait()
    arrays["cross_elem"].wait()
    cross_key = cross_face[...] * elems + cross_elem[...]
    cross_key = jnp.concatenate(
        [cross_key, jnp.full((1, lanes - slots), -1, jnp.int32)], axis=1
    )
    for face in range(6):
        rows = lax.broadcasted_iota(jnp.int32, (elems, lanes), 0) + face * elems
        hot_cross[pl.ds(face * elems, elems), :] = jnp.where(
            rows == cross_key, 1.0, 0.0
        ).astype(jnp.bfloat16)
    arrays["start"].wait()

    def prepare_inner():
        for name in ("inner_face", "inner_elem", "inner_orient", "inner_jac"):
            arrays[name].wait()
        for name in ("cross_orient", "cross_count", "cross_jac"):
            arrays[name].wait()
        inner_key = inner_face[...] * elems + inner_elem[...]
        inner_key = jnp.concatenate([inner_key[0:1], inner_key[1:2]], axis=1)
        for face in range(6):
            rows = lax.broadcasted_iota(jnp.int32, (elems, 2 * fin), 0) + face * elems
            hot_inner[pl.ds(face * elems, elems), :] = jnp.where(
                rows == inner_key, 1.0, 0.0
            ).astype(jnp.bfloat16)
        for u in range(VARS):
            for v in range(VARS):
                jac[u, v : v + 1, 0:fin] = inner_jac[5 * u + v, 0:1, :]
                jac[u, v : v + 1, fin : 2 * fin] = inner_jac[5 * u + v, 1:2, :]
                jac[u, v : v + 1, 2 * fin : 2 * fin + slots] = cross_jac[5 * u + v, :, :]
        orient = inner_orient[...]
        inner_orients = jnp.concatenate([orient, orient_back(orient)], axis=1)
        cross_orients = jnp.concatenate(
            [cross_orient[...], jnp.zeros((1, lanes - slots), jnp.int32)], axis=1
        )
        lane = lax.broadcasted_iota(jnp.int32, (1, lanes), 1)
        live = jnp.zeros((1, lanes), jnp.int32)
        for k in range(5):
            live = jnp.where((lane >= k * cap) & (lane < k * cap + cross_count[0, k]), 1, live)
        live = jnp.broadcast_to(live == 1, (8, lanes))
        return inner_orients, cross_orients, live

    for sweep in range(SWEEPS):
        for v in range(VARS):
            state[pl.ds(v, NODES, stride=8), :] = current[v * NODES : (v + 1) * NODES, :]
        peer_copies = [
            pltpu.make_async_remote_copy(
                src_ref=current,
                dst_ref=peer_buf.at[sweep, d],
                send_sem=peer_send_sem.at[sweep, d],
                recv_sem=peer_recv_sem.at[sweep, d],
                device_id={"tm": peers[d]},
                device_id_type=MESH,
            )
            for d in range(count_times - 1)
        ]
        if sweep > 0:
            for copy in peer_copies:
                copy.start()
        tiles = [
            state[8 * node : 8 * node + 8, :] * NODE_WEIGHT[node] for node in range(NODES)
        ]
        faces = jnp.concatenate(
            [
                jnp.concatenate([tiles[FACE_NODES[face][n]] for face in range(6)], axis=1)
                for n in range(9)
            ],
            axis=0,
        )
        faces = split_rows(faces)

        cross_trace = jnp.dot(faces, hot_cross[...], preferred_element_type=jnp.float32)
        cross_trace = cross_trace[0:72] + cross_trace[72:144]
        for k in range(5):
            column = (k // 4) * 128
            last = cross_trace[64:72, column : column + 128]
            last = pltpu.roll(last, -k % 4 * cap, 1) if k % 4 else last
            for h in range(2):
                packed = zero_tile
                for g in range(4):
                    n = 4 * h + g
                    piece = cross_trace[8 * n : 8 * n + 8, column : column + 128]
                    shift = (g - k % 4) * cap % 128
                    piece = pltpu.roll(piece, shift, 1) if shift else piece
                    packed = jnp.where(group == g, piece, packed)
                extra = pltpu.roll(last, 5 if h == 0 else 2, 0)
                packed = jnp.where(row >= VARS, extra, packed)
                send_buf[sweep, k, 8 * h : 8 * h + 8, :] = packed
        if sweep == 0:
            pl.semaphore_wait(barrier, 5 + count_times - 1)
        copies = [
            pltpu.make_async_remote_copy(
                src_ref=send_buf.at[sweep, k],
                dst_ref=recv_buf.at[sweep, MIRROR[k]],
                send_sem=send_sem.at[sweep, k],
                recv_sem=recv_sem.at[sweep, MIRROR[k]],
                device_id={"mesh": partners[k]},
                device_id_type=MESH,
            )
            for k in range(5)
        ]
        for k in (3, 2, 4, 0, 1):
            copies[k].start()
        if sweep == 0:
            for copy in peer_copies:
                copy.start()
            inner_orients, cross_orients, live = prepare_inner()

        trace = jnp.dot(faces, hot_inner[...], preferred_element_type=jnp.float32)
        trace = trace[0:72] + trace[72:144]
        trace = [
            jnp.concatenate(
                [trace[8 * n : 8 * n + 8, fin:], trace[8 * n : 8 * n + 8, :fin]], axis=1
            )
            for n in range(9)
        ]
        trace = apply_orient(trace, inner_orients)
        received = apply_jacobian([jac[u, :, 0 : 2 * fin] for u in range(VARS)], trace)
        received = split_rows(jnp.concatenate(received, axis=0))
        placed = lax.dot_general(
            received,
            hot_inner[...],
            (((1,), (1,)), ((), ())),
            preferred_element_type=jnp.float32,
        )
        inner_placed = placed[0:72] + placed[72:144]

        for copy in copies:
            copy.wait_recv()
        arrived = []
        for n in range(9):
            h, g = n // 4 % 2, n % 4
            columns = [zero_tile] * (lanes // 128)
            for k in range(5):
                piece = recv_buf[sweep, k, 8 * h : 8 * h + 8, :]
                if n == 8:
                    other = recv_buf[sweep, k, 8:16, :]
                    piece = jnp.where(row < 3, pltpu.roll(piece, 3, 0), pltpu.roll(other, 6, 0))
                shift = (k % 4 - g) * cap % 128
                piece = pltpu.roll(piece, shift, 1) if shift else piece
                columns[k // 4] = jnp.where(group == k % 4, piece, columns[k // 4])
            arrived.append(jnp.concatenate(columns, axis=1))
        arrived = apply_orient(arrived, cross_orients)
        received = apply_jacobian([jac[u, :, 2 * fin :] for u in range(VARS)], arrived)
        received = [jnp.where(live, value, 0.0) for value in received]
        received = split_rows(jnp.concatenate(received, axis=0))
        placed = lax.dot_general(
            received,
            hot_cross[...],
            (((1,), (1,)), ((), ())),
            preferred_element_type=jnp.float32,
        )
        placed = placed[0:72] + placed[72:144] + inner_placed

        totals = [zero_tile] * NODES
        for face in range(6):
            for n in range(9):
                node = FACE_NODES[face][n]
                totals[node] = (
                    totals[node] + placed[8 * n : 8 * n + 8, face * elems : (face + 1) * elems]
                )
        for node in range(NODES):
            couple[8 * node : 8 * node + 8, :] = totals[node]

        if sweep == 0:
            arrays["source"].wait()
            arrays["mass"].wait()
        for copy in peer_copies:
            copy.wait_recv()
        for v in range(VARS):
            rows = slice(v * NODES, (v + 1) * NODES)
            spectral = coef[1] * peer_buf[sweep, 0, rows, :]
            for d in range(1, count_times - 1):
                spectral = spectral + coef[d + 1] * peer_buf[sweep, d, rows, :]
            value = (
                source[rows, :]
                - couple[pl.ds(v, NODES, stride=8), :]
                - mass[rows, :] * spectral
            )
            resid[rows, :] = value.astype(jnp.bfloat16).astype(jnp.float32)

        for copy in peer_copies:
            copy.wait_send()
        for copy in copies:
            copy.wait_send()
        if sweep == 0:
            for load in loads:
                load.wait()
        target = out if sweep == SWEEPS - 1 else current
        top = resid[0:128, :].reshape(16, 8, 128)
        tail = resid[128:136, :]

        def row_sum(row):
            block = inv_v[row, 0:128, :].astype(jnp.float32).reshape(16, 8, 128)
            last = inv_v[row, 128:135, :].astype(jnp.float32)
            last = jnp.concatenate([last, jnp.zeros((1, 128), jnp.float32)], axis=0)
            total = jnp.sum(block * top, axis=0) + last * tail
            return jnp.sum(total, axis=0, keepdims=True)

        def body(step, carry):
            base = pl.multiple_of(step * 8, 8)
            sums = [row_sum(base + i) for i in range(8)]
            target[pl.ds(base, 8), :] = jnp.concatenate(sums, axis=0)
            return carry

        lax.fori_loop(0, 16, body, 0)
        sums = [row_sum(128 + i) for i in range(7)]
        target[128:135, :] = jnp.concatenate(sums, axis=0)


def on_device(
    inverse,
    start,
    source,
    mass,
    inner_elem,
    inner_face,
    inner_orient,
    inner_jac,
    cross_elem,
    cross_face,
    cross_orient,
    cross_count,
    cross_jac,
):
    count_times = lax.axis_size("tm")
    count_mesh = lax.axis_size("mesh")
    rows, elems = mass.shape
    fin = inner_orient.shape[0]
    slots = cross_elem.shape[1]
    lanes = -(-slots // 128) * 128
    vmem = pl.BlockSpec(memory_space=pltpu.VMEM)
    specs = [pl.BlockSpec(memory_space=pl.ANY)] * 13
    result = pl.pallas_call(
        functools.partial(kernel, count_times, count_mesh),
        out_shape=jax.ShapeDtypeStruct((rows, elems), jnp.float32),
        in_specs=specs,
        out_specs=vmem,
        scratch_shapes=[
            pltpu.VMEM((rows, elems), jnp.float32),
            pltpu.VMEM((rows, elems), jnp.float32),
            pltpu.VMEM((2, fin), jnp.int32),
            pltpu.VMEM((2, fin), jnp.int32),
            pltpu.VMEM((1, fin), jnp.int32),
            pltpu.VMEM((25, 2, fin), jnp.float32),
            pltpu.VMEM((1, slots), jnp.int32),
            pltpu.VMEM((1, slots), jnp.int32),
            pltpu.VMEM((1, slots), jnp.int32),
            pltpu.SMEM((1, 5), jnp.int32),
            pltpu.VMEM((25, 1, slots), jnp.float32),
            pltpu.VMEM((rows, rows, elems), jnp.bfloat16),
            pltpu.VMEM((6 * elems, 2 * fin), jnp.bfloat16),
            pltpu.VMEM((6 * elems, lanes), jnp.bfloat16),
            pltpu.VMEM((8 * NODES, elems), jnp.float32),
            pltpu.VMEM((VARS, 8, 2 * fin + lanes), jnp.float32),
            pltpu.VMEM((8 * NODES, elems), jnp.float32),
            pltpu.VMEM((136, elems), jnp.float32),
            pltpu.VMEM((rows, elems), jnp.float32),
            pltpu.VMEM((SWEEPS, 5, 16, 128), jnp.float32),
            pltpu.VMEM((SWEEPS, 5, 16, 128), jnp.float32),
            pltpu.VMEM((SWEEPS, count_times - 1, rows, elems), jnp.float32),
            pltpu.SemaphoreType.DMA((12,)),
            pltpu.SemaphoreType.DMA((5,)),
            pltpu.SemaphoreType.DMA((SWEEPS, 5)),
            pltpu.SemaphoreType.DMA((SWEEPS, 5)),
            pltpu.SemaphoreType.DMA((SWEEPS, count_times - 1)),
            pltpu.SemaphoreType.DMA((SWEEPS, count_times - 1)),
        ],
        compiler_params=pltpu.CompilerParams(
            collective_id=0, has_side_effects=True, vmem_limit_bytes=60 * 1024 * 1024
        ),
    )(
        inverse[0],
        jnp.transpose(start, (1, 0, 2)),
        jnp.transpose(source, (1, 0, 2)),
        mass,
        inner_elem,
        inner_face,
        inner_orient.reshape(1, fin),
        jnp.transpose(inner_jac[0], (1, 0, 2)),
        cross_elem,
        cross_face,
        cross_orient,
        cross_count,
        cross_jac[0],
    )
    return result[None]


def solution(mesh):
    in_specs = (
        P("tm", None, None, "mesh"),
        P("tm", None, "mesh"),
        P("tm", None, "mesh"),
        P(None, "mesh"),
        P(None, "mesh"),
        P(None, "mesh"),
        P("mesh"),
        P("tm", None, None, "mesh"),
        P("mesh", None),
        P("mesh", None),
        P("mesh", None),
        P("mesh", None),
        P("tm", None, "mesh", None),
    )
    out_specs = P("tm", None, "mesh")
    return jax.shard_map(
        on_device, mesh=mesh, in_specs=in_specs, out_specs=out_specs, check_vma=False
    )
```

```python
import functools
import math

import jax
import jax.numpy as jnp
import numpy as np
from jax import lax
from jax.experimental import pallas as pl
from jax.experimental.pallas import tpu as pltpu
from jax.sharding import PartitionSpec as P

SWEEPS = 2
VARS = 5
NODES = 27
MIRROR = (1, 0, 4, 3, 2)
LINE_WEIGHTS = (1.0 / 3.0, 4.0 / 3.0, 1.0 / 3.0)
MESH = pl.DeviceIdType.MESH


def face_table():
    nodes = [[0] * 9 for _ in range(6)]
    weight = [1.0] * NODES
    for face in range(6):
        normal = face // 2
        tangent = [axis for axis in range(3) if axis != normal]
        for j in range(3):
            for i in range(3):
                coords = [0, 0, 0]
                coords[normal] = 2 * (face % 2)
                coords[tangent[0]] = i
                coords[tangent[1]] = j
                node = 9 * coords[2] + 3 * coords[1] + coords[0]
                nodes[face][3 * j + i] = node
                weight[node] = float(np.float32(LINE_WEIGHTS[i] * LINE_WEIGHTS[j]))
    return nodes, weight


FACE_NODES, NODE_WEIGHT = face_table()


def coef_table(count):
    table = [0.0] * count
    for k in range(1, count):
        parity = (-1.0) ** k
        phase = math.pi * k / count
        table[k] = 0.3 * parity * math.cos(phase) / math.sin(phase) + 1.2 * parity / count
    return [float(np.float32(c)) for c in table]


def split_rows(value):
    high = value.astype(jnp.bfloat16).astype(jnp.float32)
    return jnp.concatenate([high, value - high], axis=0).astype(jnp.bfloat16)


def orient_back(orient):
    swapped = 4 + 2 * (orient & 1) + ((orient >> 1) & 1)
    return jnp.where(orient >= 4, swapped, orient)


def apply_orient(trace, orient):
    shape = trace[0].shape
    flip_i = jnp.broadcast_to((orient & 1) == 1, shape)
    flip_j = jnp.broadcast_to((orient & 2) == 2, shape)
    swap = jnp.broadcast_to(orient >= 4, shape)
    step = [
        trace[3 * j + i] if i == 1 else jnp.where(flip_i, trace[3 * j + 2 - i], trace[3 * j + i])
        for j in range(3)
        for i in range(3)
    ]
    step = [
        step[3 * j + i] if j == 1 else jnp.where(flip_j, step[3 * (2 - j) + i], step[3 * j + i])
        for j in range(3)
        for i in range(3)
    ]
    return [
        step[3 * j + i] if i == j else jnp.where(swap, step[3 * i + j], step[3 * j + i])
        for j in range(3)
        for i in range(3)
    ]


def apply_jacobian(jac, trace):
    received = []
    for value in trace:
        total = jac[0] * value[0:1, :]
        for u in range(1, VARS):
            total = total + jac[u] * value[u : u + 1, :]
        received.append(total)
    return received


def kernel(
    count_times,
    count_mesh,
    inverse,
    start_h,
    source_h,
    mass_h,
    inner_elem_h,
    inner_face_h,
    inner_orient_h,
    inner_jac_h,
    cross_elem_h,
    cross_face_h,
    cross_orient_h,
    cross_count_h,
    cross_jac_h,
    out,
    source,
    mass,
    inner_elem,
    inner_face,
    inner_orient,
    inner_jac,
    cross_elem,
    cross_face,
    cross_orient,
    cross_count,
    cross_jac,
    inv_v,
    hot_inner,
    hot_cross,
    state,
    jac,
    couple,
    resid,
    current,
    inner_orients,
    cross_orients,
    alive,
    send_buf,
    recv_buf,
    peer_buf,
    load_sem,
    inv_sem,
    send_sem,
    recv_sem,
    peer_send_sem,
    peer_recv_sem,
):
    total_rows, elems = mass.shape
    fin = inner_orient.shape[1]
    slots = cross_orient.shape[1]
    cap = slots // 5
    lanes = hot_cross.shape[1]
    chunk = total_rows // 5
    me = lax.axis_index("mesh")
    mine = lax.axis_index("tm")
    offsets = [1, count_mesh - 1, count_mesh // 2 - 1, count_mesh // 2, count_mesh // 2 + 1]
    partners = [lax.rem(me + off, count_mesh) for off in offsets]
    peers = [lax.rem(mine - d + count_times, count_times) for d in range(1, count_times)]
    coef = coef_table(count_times)

    loads = [
        pltpu.make_async_copy(
            inverse.at[pl.ds(c * chunk, chunk)], inv_v.at[pl.ds(c * chunk, chunk)], inv_sem.at[c]
        )
        for c in range(5)
    ]
    pairs = {
        "cross_face": (cross_face_h, cross_face),
        "cross_elem": (cross_elem_h, cross_elem),
        "start": (start_h.at[:, 0], current.at[pl.ds(0, total_rows)]),
        "inner_face": (inner_face_h, inner_face),
        "inner_elem": (inner_elem_h, inner_elem),
        "inner_orient": (inner_orient_h, inner_orient),
        "inner_jac": (inner_jac_h, inner_jac),
        "cross_orient": (cross_orient_h, cross_orient),
        "cross_count": (cross_count_h, cross_count),
        "cross_jac": (cross_jac_h, cross_jac),
        "source": (source_h.at[:, 0], source),
        "mass": (mass_h, mass),
    }
    arrays = {
        name: pltpu.make_async_copy(src, dst, load_sem.at[index])
        for index, (name, (src, dst)) in enumerate(pairs.items())
    }
    for load in arrays.values():
        load.start()
    for load in loads:
        load.start()

    barrier = pltpu.get_barrier_semaphore()
    for partner in partners:
        pl.semaphore_signal(barrier, inc=1, device_id={"mesh": partner}, device_id_type=MESH)
    for peer in peers:
        pl.semaphore_signal(barrier, inc=1, device_id={"tm": peer}, device_id_type=MESH)

    state[...] = jnp.zeros_like(state)
    resid[...] = jnp.zeros_like(resid)
    jac[...] = jnp.zeros_like(jac)
    zero_tile = jnp.zeros((8, 128), jnp.float32)
    group = lax.broadcasted_iota(jnp.int32, (8, 128), 1) // cap
    row = lax.broadcasted_iota(jnp.int32, (8, 128), 0)

    arrays["cross_face"].wait()
    arrays["cross_elem"].wait()
    cross_key = cross_face[...] * elems + cross_elem[...]
    cross_key = jnp.concatenate(
        [cross_key, jnp.full((1, lanes - slots), -1, jnp.int32)], axis=1
    )
    for face in range(6):
        rows = lax.broadcasted_iota(jnp.int32, (elems, lanes), 0) + face * elems
        hot_cross[pl.ds(face * elems, elems), :] = jnp.where(
            rows == cross_key, 1.0, 0.0
        ).astype(jnp.bfloat16)
    arrays["start"].wait()

    def prepare_inner():
        for name in ("inner_face", "inner_elem", "inner_orient", "inner_jac"):
            arrays[name].wait()
        for name in ("cross_orient", "cross_count", "cross_jac"):
            arrays[name].wait()
        inner_key = inner_face[...] * elems + inner_elem[...]
        inner_key = jnp.concatenate([inner_key[0:1], inner_key[1:2]], axis=1)
        for face in range(6):
            rows = lax.broadcasted_iota(jnp.int32, (elems, 2 * fin), 0) + face * elems
            hot_inner[pl.ds(face * elems, elems), :] = jnp.where(
                rows == inner_key, 1.0, 0.0
            ).astype(jnp.bfloat16)
        for u in range(VARS):
            for v in range(VARS):
                jac[u, v : v + 1, 0:fin] = inner_jac[5 * u + v, 0:1, :]
                jac[u, v : v + 1, fin : 2 * fin] = inner_jac[5 * u + v, 1:2, :]
                jac[u, v : v + 1, 2 * fin : 2 * fin + slots] = cross_jac[5 * u + v, :, :]
        orient = inner_orient[...]
        inner_orients[...] = jnp.concatenate([orient, orient_back(orient)], axis=1)
        cross_orients[...] = jnp.concatenate(
            [cross_orient[...], jnp.zeros((1, lanes - slots), jnp.int32)], axis=1
        )
        lane = lax.broadcasted_iota(jnp.int32, (1, lanes), 1)
        live = jnp.zeros((1, lanes), jnp.int32)
        for k in range(5):
            live = jnp.where((lane >= k * cap) & (lane < k * cap + cross_count[0, k]), 1, live)
        alive[...] = live

    def send_peers(sweep):
        return [
            pltpu.make_async_remote_copy(
                src_ref=current.at[pl.ds(0, total_rows)],
                dst_ref=peer_buf.at[sweep, d],
                send_sem=peer_send_sem.at[sweep, d],
                recv_sem=peer_recv_sem.at[sweep, d],
                device_id={"tm": peers[d]},
                device_id_type=MESH,
            )
            for d in range(count_times - 1)
        ]

    def one_sweep(sweep, carry):
        first = sweep == 0

        for v in range(VARS):
            state[pl.ds(v, NODES, stride=8), :] = current[v * NODES : (v + 1) * NODES, :]
        peer_copies = send_peers(sweep)
        tiles = [
            state[8 * node : 8 * node + 8, :] * NODE_WEIGHT[node] for node in range(NODES)
        ]
        faces = jnp.concatenate(
            [
                jnp.concatenate([tiles[FACE_NODES[face][n]] for face in range(6)], axis=1)
                for n in range(9)
            ],
            axis=0,
        )
        faces = split_rows(faces)

        cross_trace = jnp.dot(faces, hot_cross[...], preferred_element_type=jnp.float32)
        cross_trace = cross_trace[0:72] + cross_trace[72:144]
        for k in range(5):
            column = (k // 4) * 128
            last = cross_trace[64:72, column : column + 128]
            last = pltpu.roll(last, -k % 4 * cap, 1) if k % 4 else last
            for h in range(2):
                packed = zero_tile
                for g in range(4):
                    n = 4 * h + g
                    piece = cross_trace[8 * n : 8 * n + 8, column : column + 128]
                    shift = (g - k % 4) * cap % 128
                    piece = pltpu.roll(piece, shift, 1) if shift else piece
                    packed = jnp.where(group == g, piece, packed)
                extra = pltpu.roll(last, 5 if h == 0 else 2, 0)
                packed = jnp.where(row >= VARS, extra, packed)
                send_buf[sweep, k, 8 * h : 8 * h + 8, :] = packed

        @pl.when(first)
        def _():
            pl.semaphore_wait(barrier, 5 + count_times - 1)

        copies = [
            pltpu.make_async_remote_copy(
                src_ref=send_buf.at[sweep, k],
                dst_ref=recv_buf.at[sweep, MIRROR[k]],
                send_sem=send_sem.at[sweep, k],
                recv_sem=recv_sem.at[sweep, MIRROR[k]],
                device_id={"mesh": partners[k]},
                device_id_type=MESH,
            )
            for k in range(5)
        ]
        for k in (3, 2, 4, 0, 1):
            copies[k].start()

        @pl.when(first)
        def _():
            for copy in peer_copies:
                copy.start()
            prepare_inner()

        trace = jnp.dot(faces, hot_inner[...], preferred_element_type=jnp.float32)
        trace = trace[0:72] + trace[72:144]
        trace = [
            jnp.concatenate(
                [trace[8 * n : 8 * n + 8, fin:], trace[8 * n : 8 * n + 8, :fin]], axis=1
            )
            for n in range(9)
        ]
        trace = apply_orient(trace, inner_orients[...])
        received = apply_jacobian([jac[u, :, 0 : 2 * fin] for u in range(VARS)], trace)
        received = split_rows(jnp.concatenate(received, axis=0))
        placed = lax.dot_general(
            received,
            hot_inner[...],
            (((1,), (1,)), ((), ())),
            preferred_element_type=jnp.float32,
        )
        inner_placed = placed[0:72] + placed[72:144]

        for copy in copies:
            copy.wait_recv()
        arrived = []
        for n in range(9):
            h, g = n // 4 % 2, n % 4
            columns = [zero_tile] * (lanes // 128)
            for k in range(5):
                piece = recv_buf[sweep, k, 8 * h : 8 * h + 8, :]
                if n == 8:
                    other = recv_buf[sweep, k, 8:16, :]
                    piece = jnp.where(row < 3, pltpu.roll(piece, 3, 0), pltpu.roll(other, 6, 0))
                shift = (k % 4 - g) * cap % 128
                piece = pltpu.roll(piece, shift, 1) if shift else piece
                columns[k // 4] = jnp.where(group == k % 4, piece, columns[k // 4])
            arrived.append(jnp.concatenate(columns, axis=1))
        arrived = apply_orient(arrived, cross_orients[...])
        received = apply_jacobian([jac[u, :, 2 * fin :] for u in range(VARS)], arrived)
        live = jnp.broadcast_to(alive[...] == 1, (8, lanes))
        received = [jnp.where(live, value, 0.0) for value in received]
        received = split_rows(jnp.concatenate(received, axis=0))
        placed = lax.dot_general(
            received,
            hot_cross[...],
            (((1,), (1,)), ((), ())),
            preferred_element_type=jnp.float32,
        )
        placed = placed[0:72] + placed[72:144] + inner_placed

        totals = [zero_tile] * NODES
        for face in range(6):
            for n in range(9):
                node = FACE_NODES[face][n]
                totals[node] = (
                    totals[node] + placed[8 * n : 8 * n + 8, face * elems : (face + 1) * elems]
                )
        for node in range(NODES):
            couple[8 * node : 8 * node + 8, :] = totals[node]


        @pl.when(first)
        def _():
            arrays["source"].wait()
            arrays["mass"].wait()
        for copy in peer_copies:
            copy.wait_recv()
        for v in range(VARS):
            rows = slice(v * NODES, (v + 1) * NODES)
            spectral = coef[1] * peer_buf[sweep, 0, rows, :]
            for d in range(1, count_times - 1):
                spectral = spectral + coef[d + 1] * peer_buf[sweep, d, rows, :]
            value = (
                source[rows, :]
                - couple[pl.ds(v, NODES, stride=8), :]
                - mass[rows, :] * spectral
            )
            resid[rows, :] = value.astype(jnp.bfloat16).astype(jnp.float32)

        for copy in peer_copies:
            copy.wait_send()
        for copy in copies:
            copy.wait_send()

        @pl.when(first)
        def _():
            for load in loads:
                load.wait()

        top = resid[0:128, :].reshape(16, 8, 128)
        tail = resid[128:136, :]

        def row_sum(row):
            block = inv_v[row, 0:128, :].astype(jnp.float32).reshape(16, 8, 128)
            last = inv_v[row, 128:135, :].astype(jnp.float32)
            last = jnp.concatenate([last, jnp.zeros((1, 128), jnp.float32)], axis=0)
            total = jnp.sum(block * top, axis=0) + last * tail
            return jnp.sum(total, axis=0, keepdims=True)

        def body(step, carry):
            base = pl.multiple_of(step * 8, 8)
            sums = [row_sum(base + i) for i in range(8)]
            current[pl.ds(base, 8), :] = jnp.concatenate(sums, axis=0)
            return carry

        lax.fori_loop(0, (total_rows + 1) // 8, body, 0)

        @pl.when(sweep < SWEEPS - 1)
        def _():
            for copy in send_peers(sweep + 1):
                copy.start()

        return carry

    lax.fori_loop(0, SWEEPS, one_sweep, 0)
    out[...] = current[0:total_rows, :]


def on_device(
    inverse,
    start,
    source,
    mass,
    inner_elem,
    inner_face,
    inner_orient,
    inner_jac,
    cross_elem,
    cross_face,
    cross_orient,
    cross_count,
    cross_jac,
):
    count_times = lax.axis_size("tm")
    count_mesh = lax.axis_size("mesh")
    rows, elems = mass.shape
    fin = inner_orient.shape[0]
    slots = cross_elem.shape[1]
    lanes = -(-slots // 128) * 128
    vmem = pl.BlockSpec(memory_space=pltpu.VMEM)
    specs = [pl.BlockSpec(memory_space=pltpu.HBM)] * 13
    result = pl.pallas_call(
        functools.partial(kernel, count_times, count_mesh),
        out_shape=jax.ShapeDtypeStruct((rows, elems), jnp.float32),
        in_specs=specs,
        out_specs=vmem,
        scratch_shapes=[
            pltpu.VMEM((rows, elems), jnp.float32),
            pltpu.VMEM((rows, elems), jnp.float32),
            pltpu.VMEM((2, fin), jnp.int32),
            pltpu.VMEM((2, fin), jnp.int32),
            pltpu.VMEM((1, fin), jnp.int32),
            pltpu.VMEM((25, 2, fin), jnp.float32),
            pltpu.VMEM((1, slots), jnp.int32),
            pltpu.VMEM((1, slots), jnp.int32),
            pltpu.VMEM((1, slots), jnp.int32),
            pltpu.SMEM((1, 5), jnp.int32),
            pltpu.VMEM((25, 1, slots), jnp.float32),
            pltpu.VMEM((rows + 1, rows, elems), jnp.bfloat16),
            pltpu.VMEM((6 * elems, 2 * fin), jnp.bfloat16),
            pltpu.VMEM((6 * elems, lanes), jnp.bfloat16),
            pltpu.VMEM((8 * NODES, elems), jnp.float32),
            pltpu.VMEM((VARS, 8, 2 * fin + lanes), jnp.float32),
            pltpu.VMEM((8 * NODES, elems), jnp.float32),
            pltpu.VMEM((rows + 1, elems), jnp.float32),
            pltpu.VMEM((rows + 1, elems), jnp.float32),
            pltpu.VMEM((1, 2 * fin), jnp.int32),
            pltpu.VMEM((1, lanes), jnp.int32),
            pltpu.VMEM((1, lanes), jnp.int32),
            pltpu.VMEM((SWEEPS, 5, 16, 128), jnp.float32),
            pltpu.VMEM((SWEEPS, 5, 16, 128), jnp.float32),
            pltpu.VMEM((SWEEPS, count_times - 1, rows, elems), jnp.float32),
            pltpu.SemaphoreType.DMA((12,)),
            pltpu.SemaphoreType.DMA((5,)),
            pltpu.SemaphoreType.DMA((SWEEPS, 5)),
            pltpu.SemaphoreType.DMA((SWEEPS, 5)),
            pltpu.SemaphoreType.DMA((SWEEPS, count_times - 1)),
            pltpu.SemaphoreType.DMA((SWEEPS, count_times - 1)),
        ],
        compiler_params=pltpu.CompilerParams(
            collective_id=0, has_side_effects=True, vmem_limit_bytes=32 * 1024 * 1024
        ),
    )(
        *[
            pltpu.with_memory_space_constraint(operand, pltpu.HBM)
            for operand in (
                inverse[0],
                jnp.transpose(start, (1, 0, 2)),
                jnp.transpose(source, (1, 0, 2)),
                mass,
                inner_elem,
                inner_face,
                inner_orient.reshape(1, fin),
                jnp.transpose(inner_jac[0], (1, 0, 2)),
                cross_elem,
                cross_face,
                cross_orient,
                cross_count,
                cross_jac[0],
            )
        ]
    )
    return result[None]


def solution(mesh):
    in_specs = (
        P("tm", None, None, "mesh"),
        P("tm", None, "mesh"),
        P("tm", None, "mesh"),
        P(None, "mesh"),
        P(None, "mesh"),
        P(None, "mesh"),
        P("mesh"),
        P("tm", None, None, "mesh"),
        P("mesh", None),
        P("mesh", None),
        P("mesh", None),
        P("mesh", None),
        P("tm", None, "mesh", None),
    )
    out_specs = P("tm", None, "mesh")
    return jax.shard_map(
        on_device, mesh=mesh, in_specs=in_specs, out_specs=out_specs, check_vma=False
    )
```

```python
import functools
import math

import jax
import jax.numpy as jnp
import numpy as np
from jax import lax
from jax.experimental import pallas as pl
from jax.experimental.pallas import tpu as pltpu
from jax.sharding import PartitionSpec as P

SWEEPS = 2
VARS = 5
NODES = 27
MIRROR = (1, 0, 4, 3, 2)
LINE_WEIGHTS = (1.0 / 3.0, 4.0 / 3.0, 1.0 / 3.0)
MESH = pl.DeviceIdType.MESH


def face_table():
    nodes = [[0] * 9 for _ in range(6)]
    weight = [1.0] * NODES
    for face in range(6):
        normal = face // 2
        tangent = [axis for axis in range(3) if axis != normal]
        for j in range(3):
            for i in range(3):
                coords = [0, 0, 0]
                coords[normal] = 2 * (face % 2)
                coords[tangent[0]] = i
                coords[tangent[1]] = j
                node = 9 * coords[2] + 3 * coords[1] + coords[0]
                nodes[face][3 * j + i] = node
                weight[node] = float(np.float32(LINE_WEIGHTS[i] * LINE_WEIGHTS[j]))
    return nodes, weight


FACE_NODES, NODE_WEIGHT = face_table()


def coef_table(count):
    table = [0.0] * count
    for k in range(1, count):
        parity = (-1.0) ** k
        phase = math.pi * k / count
        table[k] = 0.3 * parity * math.cos(phase) / math.sin(phase) + 1.2 * parity / count
    return [float(np.float32(c)) for c in table]


def split_rows(value):
    high = value.astype(jnp.bfloat16).astype(jnp.float32)
    return jnp.concatenate([high, value - high], axis=0).astype(jnp.bfloat16)


def orient_back(orient):
    swapped = 4 + 2 * (orient & 1) + ((orient >> 1) & 1)
    return jnp.where(orient >= 4, swapped, orient)


def apply_orient(trace, orient):
    shape = trace[0].shape
    flip_i = jnp.broadcast_to((orient & 1) == 1, shape)
    flip_j = jnp.broadcast_to((orient & 2) == 2, shape)
    swap = jnp.broadcast_to(orient >= 4, shape)
    step = [
        trace[3 * j + i] if i == 1 else jnp.where(flip_i, trace[3 * j + 2 - i], trace[3 * j + i])
        for j in range(3)
        for i in range(3)
    ]
    step = [
        step[3 * j + i] if j == 1 else jnp.where(flip_j, step[3 * (2 - j) + i], step[3 * j + i])
        for j in range(3)
        for i in range(3)
    ]
    return [
        step[3 * j + i] if i == j else jnp.where(swap, step[3 * i + j], step[3 * j + i])
        for j in range(3)
        for i in range(3)
    ]


def apply_jacobian(jac, trace):
    received = []
    for value in trace:
        total = jac[0] * value[0:1, :]
        for u in range(1, VARS):
            total = total + jac[u] * value[u : u + 1, :]
        received.append(total)
    return received


def node_sums(placed):
    totals = [None] * NODES
    for face in range(6):
        for n in range(9):
            node = FACE_NODES[face][n]
            piece = placed[8 * n : 8 * n + 8, face * 128 : (face + 1) * 128]
            totals[node] = piece if totals[node] is None else totals[node] + piece
    zero = jnp.zeros((8, 128), jnp.float32)
    return [zero if total is None else total for total in totals]


def kernel(
    count_times,
    count_mesh,
    inverse,
    start_h,
    source_h,
    mass_h,
    inner_elem_h,
    inner_face_h,
    inner_orient_h,
    inner_jac_h,
    cross_elem_h,
    cross_face_h,
    cross_orient_h,
    cross_count_h,
    cross_jac_h,
    out,
    source,
    mass,
    inner_elem,
    inner_face,
    inner_orient,
    inner_jac,
    cross_elem,
    cross_face,
    cross_orient,
    cross_count,
    cross_jac,
    inv_v,
    hot_inner,
    hot_cross,
    state,
    jac,
    couple,
    resid,
    current,
    inner_orients,
    cross_orients,
    alive,
    partial,
    send_buf,
    recv_buf,
    peer_buf,
    load_sem,
    inv_sem,
    send_sem,
    recv_sem,
    peer_send_sem,
    peer_recv_sem,
):
    total_rows, elems = mass.shape
    fin = inner_orient.shape[1]
    slots = cross_orient.shape[1]
    cap = slots // 5
    lanes = hot_cross.shape[1]
    chunk = total_rows // 5
    me = lax.axis_index("mesh")
    mine = lax.axis_index("tm")
    offsets = [1, count_mesh - 1, count_mesh // 2 - 1, count_mesh // 2, count_mesh // 2 + 1]
    partners = [lax.rem(me + off, count_mesh) for off in offsets]
    peers = [lax.rem(mine - d + count_times, count_times) for d in range(1, count_times)]
    coef = coef_table(count_times)

    loads = [
        pltpu.make_async_copy(
            inverse.at[pl.ds(c * chunk, chunk)], inv_v.at[pl.ds(c * chunk, chunk)], inv_sem.at[c]
        )
        for c in range(5)
    ]
    pairs = {
        "cross_face": (cross_face_h, cross_face),
        "cross_elem": (cross_elem_h, cross_elem),
        "start": (start_h.at[:, 0], current.at[pl.ds(0, total_rows)]),
        "inner_face": (inner_face_h, inner_face),
        "inner_elem": (inner_elem_h, inner_elem),
        "inner_orient": (inner_orient_h, inner_orient),
        "inner_jac": (inner_jac_h, inner_jac),
        "cross_orient": (cross_orient_h, cross_orient),
        "cross_count": (cross_count_h, cross_count),
        "cross_jac": (cross_jac_h, cross_jac),
        "source": (source_h.at[:, 0], source),
        "mass": (mass_h, mass),
    }
    arrays = {
        name: pltpu.make_async_copy(src, dst, load_sem.at[index])
        for index, (name, (src, dst)) in enumerate(pairs.items())
    }
    for name in ("cross_face", "cross_elem", "start"):
        arrays[name].start()

    barrier = pltpu.get_barrier_semaphore()
    for partner in partners:
        pl.semaphore_signal(barrier, inc=1, device_id={"mesh": partner}, device_id_type=MESH)
    for peer in peers:
        pl.semaphore_signal(barrier, inc=1, device_id={"tm": peer}, device_id_type=MESH)
    for name in list(arrays)[3:]:
        arrays[name].start()
    for load in loads:
        load.start()

    state[...] = jnp.zeros_like(state)
    resid[...] = jnp.zeros_like(resid)
    jac[...] = jnp.zeros_like(jac)
    zero_tile = jnp.zeros((8, 128), jnp.float32)
    group = lax.broadcasted_iota(jnp.int32, (8, 128), 1) // cap
    row = lax.broadcasted_iota(jnp.int32, (8, 128), 0)

    arrays["cross_face"].wait()
    arrays["cross_elem"].wait()
    cross_key = cross_face[...] * elems + cross_elem[...]
    cross_key = jnp.concatenate(
        [cross_key, jnp.full((1, lanes - slots), -1, jnp.int32)], axis=1
    )
    for face in range(6):
        rows = lax.broadcasted_iota(jnp.int32, (elems, lanes), 0) + face * elems
        hot_cross[pl.ds(face * elems, elems), :] = jnp.where(
            rows == cross_key, 1.0, 0.0
        ).astype(jnp.bfloat16)
    arrays["start"].wait()

    def prepare_inner():
        for name in ("inner_face", "inner_elem", "inner_orient", "inner_jac"):
            arrays[name].wait()
        for name in ("cross_orient", "cross_count", "cross_jac"):
            arrays[name].wait()
        inner_key = inner_face[...] * elems + inner_elem[...]
        inner_key = jnp.concatenate([inner_key[0:1], inner_key[1:2]], axis=1)
        for face in range(6):
            rows = lax.broadcasted_iota(jnp.int32, (elems, 2 * fin), 0) + face * elems
            hot_inner[pl.ds(face * elems, elems), :] = jnp.where(
                rows == inner_key, 1.0, 0.0
            ).astype(jnp.bfloat16)
        for u in range(VARS):
            for v in range(VARS):
                jac[u, v : v + 1, 0:fin] = inner_jac[5 * u + v, 0:1, :]
                jac[u, v : v + 1, fin : 2 * fin] = inner_jac[5 * u + v, 1:2, :]
                jac[u, v : v + 1, 2 * fin : 2 * fin + slots] = cross_jac[5 * u + v, :, :]
        orient = inner_orient[...]
        inner_orients[...] = jnp.concatenate([orient, orient_back(orient)], axis=1)
        cross_orients[...] = jnp.concatenate(
            [cross_orient[...], jnp.zeros((1, lanes - slots), jnp.int32)], axis=1
        )
        lane = lax.broadcasted_iota(jnp.int32, (1, lanes), 1)
        live = jnp.zeros((1, lanes), jnp.int32)
        for k in range(5):
            live = jnp.where((lane >= k * cap) & (lane < k * cap + cross_count[0, k]), 1, live)
        alive[...] = live

    def send_peers(sweep):
        return [
            pltpu.make_async_remote_copy(
                src_ref=current.at[pl.ds(0, total_rows)],
                dst_ref=peer_buf.at[sweep, d],
                send_sem=peer_send_sem.at[sweep, d],
                recv_sem=peer_recv_sem.at[sweep, d],
                device_id={"tm": peers[d]},
                device_id_type=MESH,
            )
            for d in range(count_times - 1)
        ]

    def one_sweep(sweep, carry):
        first = sweep == 0

        for v in range(VARS):
            state[pl.ds(v, NODES, stride=8), :] = current[v * NODES : (v + 1) * NODES, :]
        peer_copies = send_peers(sweep)
        tiles = [
            state[8 * node : 8 * node + 8, :] * NODE_WEIGHT[node] for node in range(NODES)
        ]
        faces = jnp.concatenate(
            [
                jnp.concatenate([tiles[FACE_NODES[face][n]] for face in range(6)], axis=1)
                for n in range(9)
            ],
            axis=0,
        )
        faces = split_rows(faces)

        cross_trace = jnp.dot(faces, hot_cross[...], preferred_element_type=jnp.float32)
        cross_trace = cross_trace[0:72] + cross_trace[72:144]
        for k in range(5):
            column = (k // 4) * 128
            last = cross_trace[64:72, column : column + 128]
            last = pltpu.roll(last, -k % 4 * cap, 1) if k % 4 else last
            for h in range(2):
                packed = zero_tile
                for g in range(4):
                    n = 4 * h + g
                    piece = cross_trace[8 * n : 8 * n + 8, column : column + 128]
                    shift = (g - k % 4) * cap % 128
                    piece = pltpu.roll(piece, shift, 1) if shift else piece
                    packed = jnp.where(group == g, piece, packed)
                extra = pltpu.roll(last, 5 if h == 0 else 2, 0)
                packed = jnp.where(row >= VARS, extra, packed)
                send_buf[sweep, k, 8 * h : 8 * h + 8, :] = packed

        @pl.when(first)
        def _():
            pl.semaphore_wait(barrier, 5 + count_times - 1)

        copies = [
            pltpu.make_async_remote_copy(
                src_ref=send_buf.at[sweep, k],
                dst_ref=recv_buf.at[sweep, MIRROR[k]],
                send_sem=send_sem.at[sweep, k],
                recv_sem=recv_sem.at[sweep, MIRROR[k]],
                device_id={"mesh": partners[k]},
                device_id_type=MESH,
            )
            for k in range(5)
        ]
        for k in (3, 2, 4, 0, 1):
            copies[k].start()

        @pl.when(first)
        def _():
            for copy in peer_copies:
                copy.start()
            prepare_inner()

        trace = jnp.dot(faces, hot_inner[...], preferred_element_type=jnp.float32)
        trace = trace[0:72] + trace[72:144]
        trace = [
            jnp.concatenate(
                [trace[8 * n : 8 * n + 8, fin:], trace[8 * n : 8 * n + 8, :fin]], axis=1
            )
            for n in range(9)
        ]
        trace = apply_orient(trace, inner_orients[...])
        received = apply_jacobian([jac[u, :, 0 : 2 * fin] for u in range(VARS)], trace)
        received = split_rows(jnp.concatenate(received, axis=0))
        placed = lax.dot_general(
            received,
            hot_inner[...],
            (((1,), (1,)), ((), ())),
            preferred_element_type=jnp.float32,
        )
        placed = placed[0:72] + placed[72:144]
        for node, total in enumerate(node_sums(placed)):
            couple[8 * node : 8 * node + 8, :] = total

        @pl.when(first)
        def _():
            arrays["source"].wait()
            arrays["mass"].wait()

        for v in range(VARS):
            rows = slice(v * NODES, (v + 1) * NODES)
            resid[rows, :] = source[rows, :] - couple[pl.ds(v, NODES, stride=8), :]

        for copy in copies:
            copy.wait_recv()
        arrived = []
        for n in range(9):
            h, g = n // 4 % 2, n % 4
            columns = [zero_tile] * (lanes // 128)
            for k in range(5):
                piece = recv_buf[sweep, k, 8 * h : 8 * h + 8, :]
                if n == 8:
                    other = recv_buf[sweep, k, 8:16, :]
                    piece = jnp.where(row < 3, pltpu.roll(piece, 3, 0), pltpu.roll(other, 6, 0))
                shift = (k % 4 - g) * cap % 128
                piece = pltpu.roll(piece, shift, 1) if shift else piece
                columns[k // 4] = jnp.where(group == k % 4, piece, columns[k // 4])
            arrived.append(jnp.concatenate(columns, axis=1))
        arrived = apply_orient(arrived, cross_orients[...])
        received = apply_jacobian([jac[u, :, 2 * fin :] for u in range(VARS)], arrived)
        live = jnp.broadcast_to(alive[...] == 1, (8, lanes))
        received = [jnp.where(live, value, 0.0) for value in received]
        received = split_rows(jnp.concatenate(received, axis=0))
        placed = lax.dot_general(
            received,
            hot_cross[...],
            (((1,), (1,)), ((), ())),
            preferred_element_type=jnp.float32,
        )
        placed = placed[0:72] + placed[72:144]
        for node, total in enumerate(node_sums(placed)):
            couple[8 * node : 8 * node + 8, :] = total

        for copy in peer_copies:
            copy.wait_recv()
        for v in range(VARS):
            rows = slice(v * NODES, (v + 1) * NODES)
            spectral = coef[1] * peer_buf[sweep, 0, rows, :]
            for d in range(1, count_times - 1):
                spectral = spectral + coef[d + 1] * peer_buf[sweep, d, rows, :]
            value = (
                resid[rows, :]
                - couple[pl.ds(v, NODES, stride=8), :]
                - mass[rows, :] * spectral
            )
            resid[rows, :] = value.astype(jnp.bfloat16).astype(jnp.float32)

        for copy in peer_copies:
            copy.wait_send()
        for copy in copies:
            copy.wait_send()

        @pl.when(first)
        def _():
            for load in loads:
                load.wait()

        top = resid[0:128, :].reshape(16, 8, 128)
        tail = resid[128:136, :]

        def row_sum(row):
            block = inv_v[row, 0:128, :].astype(jnp.float32).reshape(16, 8, 128)
            last = inv_v[row, 128:135, :].astype(jnp.float32)
            last = jnp.concatenate([last, jnp.zeros((1, 128), jnp.float32)], axis=0)
            return jnp.sum(block * top, axis=0) + last * tail

        def body(step, carry):
            for i in range(17):
                index = step * 17 + i
                partial[pl.ds(pl.multiple_of(index * 8, 8), 8), :] = row_sum(index)
            return carry

        padded = total_rows + 1
        lax.fori_loop(0, padded // 17, body, 0)
        total = partial[pl.ds(0, padded, stride=8), :]
        for i in range(1, 8):
            total = total + partial[pl.ds(i, padded, stride=8), :]
        current[...] = total

        @pl.when(sweep < SWEEPS - 1)
        def _():
            for copy in send_peers(sweep + 1):
                copy.start()

        return carry

    lax.fori_loop(0, SWEEPS, one_sweep, 0)
    out[...] = current[0:total_rows, :]


def on_device(
    inverse,
    start,
    source,
    mass,
    inner_elem,
    inner_face,
    inner_orient,
    inner_jac,
    cross_elem,
    cross_face,
    cross_orient,
    cross_count,
    cross_jac,
):
    count_times = lax.axis_size("tm")
    count_mesh = lax.axis_size("mesh")
    rows, elems = mass.shape
    fin = inner_orient.shape[0]
    slots = cross_elem.shape[1]
    lanes = -(-slots // 128) * 128
    vmem = pl.BlockSpec(memory_space=pltpu.VMEM)
    specs = [pl.BlockSpec(memory_space=pltpu.HBM)] * 13
    result = pl.pallas_call(
        functools.partial(kernel, count_times, count_mesh),
        out_shape=jax.ShapeDtypeStruct((rows, elems), jnp.float32),
        in_specs=specs,
        out_specs=vmem,
        scratch_shapes=[
            pltpu.VMEM((rows, elems), jnp.float32),
            pltpu.VMEM((rows, elems), jnp.float32),
            pltpu.VMEM((2, fin), jnp.int32),
            pltpu.VMEM((2, fin), jnp.int32),
            pltpu.VMEM((1, fin), jnp.int32),
            pltpu.VMEM((25, 2, fin), jnp.float32),
            pltpu.VMEM((1, slots), jnp.int32),
            pltpu.VMEM((1, slots), jnp.int32),
            pltpu.VMEM((1, slots), jnp.int32),
            pltpu.SMEM((1, 5), jnp.int32),
            pltpu.VMEM((25, 1, slots), jnp.float32),
            pltpu.VMEM((rows + 1, rows, elems), jnp.bfloat16),
            pltpu.VMEM((6 * elems, 2 * fin), jnp.bfloat16),
            pltpu.VMEM((6 * elems, lanes), jnp.bfloat16),
            pltpu.VMEM((8 * NODES, elems), jnp.float32),
            pltpu.VMEM((VARS, 8, 2 * fin + lanes), jnp.float32),
            pltpu.VMEM((8 * NODES, elems), jnp.float32),
            pltpu.VMEM((rows + 1, elems), jnp.float32),
            pltpu.VMEM((rows + 1, elems), jnp.float32),
            pltpu.VMEM((1, 2 * fin), jnp.int32),
            pltpu.VMEM((1, lanes), jnp.int32),
            pltpu.VMEM((1, lanes), jnp.int32),
            pltpu.VMEM((8 * (rows + 1), elems), jnp.float32),
            pltpu.VMEM((SWEEPS, 5, 16, 128), jnp.float32),
            pltpu.VMEM((SWEEPS, 5, 16, 128), jnp.float32),
            pltpu.VMEM((SWEEPS, count_times - 1, rows, elems), jnp.float32),
            pltpu.SemaphoreType.DMA((12,)),
            pltpu.SemaphoreType.DMA((5,)),
            pltpu.SemaphoreType.DMA((SWEEPS, 5)),
            pltpu.SemaphoreType.DMA((SWEEPS, 5)),
            pltpu.SemaphoreType.DMA((SWEEPS, count_times - 1)),
            pltpu.SemaphoreType.DMA((SWEEPS, count_times - 1)),
        ],
        compiler_params=pltpu.CompilerParams(
            collective_id=0, has_side_effects=True, vmem_limit_bytes=32 * 1024 * 1024
        ),
    )(
        *[
            pltpu.with_memory_space_constraint(operand, pltpu.HBM)
            for operand in (
                inverse[0],
                jnp.transpose(start, (1, 0, 2)),
                jnp.transpose(source, (1, 0, 2)),
                mass,
                inner_elem,
                inner_face,
                inner_orient.reshape(1, fin),
                jnp.transpose(inner_jac[0], (1, 0, 2)),
                cross_elem,
                cross_face,
                cross_orient,
                cross_count,
                cross_jac[0],
            )
        ]
    )
    return result[None]


def solution(mesh):
    in_specs = (
        P("tm", None, None, "mesh"),
        P("tm", None, "mesh"),
        P("tm", None, "mesh"),
        P(None, "mesh"),
        P(None, "mesh"),
        P(None, "mesh"),
        P("mesh"),
        P("tm", None, None, "mesh"),
        P("mesh", None),
        P("mesh", None),
        P("mesh", None),
        P("mesh", None),
        P("tm", None, "mesh", None),
    )
    out_specs = P("tm", None, "mesh")
    return jax.shard_map(
        on_device, mesh=mesh, in_specs=in_specs, out_specs=out_specs, check_vma=False
    )
```

```python
import functools
import math

import jax
import jax.numpy as jnp
import numpy as np
from jax import lax
from jax.experimental import pallas as pl
from jax.experimental.pallas import tpu as pltpu
from jax.sharding import PartitionSpec as P

SWEEPS = 2
VARS = 5
NODES = 27
MIRROR = (1, 0, 4, 3, 2)
LINE_WEIGHTS = (1.0 / 3.0, 4.0 / 3.0, 1.0 / 3.0)
MESH = pl.DeviceIdType.MESH


def face_table():
    nodes = [[0] * 9 for _ in range(6)]
    weight = [1.0] * NODES
    for face in range(6):
        normal = face // 2
        tangent = [axis for axis in range(3) if axis != normal]
        for j in range(3):
            for i in range(3):
                coords = [0, 0, 0]
                coords[normal] = 2 * (face % 2)
                coords[tangent[0]] = i
                coords[tangent[1]] = j
                node = 9 * coords[2] + 3 * coords[1] + coords[0]
                nodes[face][3 * j + i] = node
                weight[node] = float(np.float32(LINE_WEIGHTS[i] * LINE_WEIGHTS[j]))
    return nodes, weight


FACE_NODES, NODE_WEIGHT = face_table()


def coef_table(count):
    table = [0.0] * count
    for k in range(1, count):
        parity = (-1.0) ** k
        phase = math.pi * k / count
        table[k] = 0.3 * parity * math.cos(phase) / math.sin(phase) + 1.2 * parity / count
    return [float(np.float32(c)) for c in table]


def split_rows(value):
    high = value.astype(jnp.bfloat16).astype(jnp.float32)
    return jnp.concatenate([high, value - high], axis=0).astype(jnp.bfloat16)


def orient_back(orient):
    swapped = 4 + 2 * (orient & 1) + ((orient >> 1) & 1)
    return jnp.where(orient >= 4, swapped, orient)


def apply_orient(trace, orient):
    shape = trace[0].shape
    flip_i = jnp.broadcast_to((orient & 1) == 1, shape)
    flip_j = jnp.broadcast_to((orient & 2) == 2, shape)
    swap = jnp.broadcast_to(orient >= 4, shape)
    step = [
        trace[3 * j + i] if i == 1 else jnp.where(flip_i, trace[3 * j + 2 - i], trace[3 * j + i])
        for j in range(3)
        for i in range(3)
    ]
    step = [
        step[3 * j + i] if j == 1 else jnp.where(flip_j, step[3 * (2 - j) + i], step[3 * j + i])
        for j in range(3)
        for i in range(3)
    ]
    return [
        step[3 * j + i] if i == j else jnp.where(swap, step[3 * i + j], step[3 * j + i])
        for j in range(3)
        for i in range(3)
    ]


def apply_jacobian(jac, trace):
    received = []
    for value in trace:
        total = jac[0] * value[0:1, :]
        for u in range(1, VARS):
            total = total + jac[u] * value[u : u + 1, :]
        received.append(total)
    return received


def node_sums(placed):
    totals = [None] * NODES
    for face in range(6):
        for n in range(9):
            node = FACE_NODES[face][n]
            piece = placed[8 * n : 8 * n + 8, face * 128 : (face + 1) * 128]
            totals[node] = piece if totals[node] is None else totals[node] + piece
    zero = jnp.zeros((8, 128), jnp.float32)
    return [zero if total is None else total for total in totals]


def kernel(
    count_times,
    count_mesh,
    inverse,
    start_h,
    source_h,
    mass_h,
    inner_elem_h,
    inner_face_h,
    inner_orient_h,
    inner_jac_h,
    cross_elem_h,
    cross_face_h,
    cross_orient_h,
    cross_count_h,
    cross_jac_h,
    out,
    source,
    mass,
    inner_elem,
    inner_face,
    inner_orient,
    inner_jac,
    cross_elem,
    cross_face,
    cross_orient,
    cross_count,
    cross_jac,
    inv_v,
    hot_inner,
    hot_cross,
    put_inner,
    put_cross,
    state,
    jac,
    couple,
    resid,
    current,
    inner_orients,
    cross_orients,
    alive,
    partial,
    send_buf,
    recv_buf,
    peer_buf,
    load_sem,
    inv_sem,
    send_sem,
    recv_sem,
    peer_send_sem,
    peer_recv_sem,
):
    total_rows, elems = mass.shape
    fin = inner_orient.shape[1]
    slots = cross_orient.shape[1]
    cap = slots // 5
    lanes = hot_cross.shape[1]
    chunk = total_rows // 5
    me = lax.axis_index("mesh")
    mine = lax.axis_index("tm")
    offsets = [1, count_mesh - 1, count_mesh // 2 - 1, count_mesh // 2, count_mesh // 2 + 1]
    partners = [lax.rem(me + off, count_mesh) for off in offsets]
    peers = [lax.rem(mine - d + count_times, count_times) for d in range(1, count_times)]
    coef = coef_table(count_times)

    loads = [
        pltpu.make_async_copy(
            inverse.at[pl.ds(c * chunk, chunk)], inv_v.at[pl.ds(c * chunk, chunk)], inv_sem.at[c]
        )
        for c in range(5)
    ]
    pairs = {
        "cross_face": (cross_face_h, cross_face),
        "cross_elem": (cross_elem_h, cross_elem),
        "start": (start_h.at[:, 0], current.at[pl.ds(0, total_rows)]),
        "inner_face": (inner_face_h, inner_face),
        "inner_elem": (inner_elem_h, inner_elem),
        "inner_orient": (inner_orient_h, inner_orient),
        "inner_jac": (inner_jac_h, inner_jac),
        "cross_orient": (cross_orient_h, cross_orient),
        "cross_count": (cross_count_h, cross_count),
        "cross_jac": (cross_jac_h, cross_jac),
        "source": (source_h.at[:, 0], source),
        "mass": (mass_h, mass),
    }
    arrays = {
        name: pltpu.make_async_copy(src, dst, load_sem.at[index])
        for index, (name, (src, dst)) in enumerate(pairs.items())
    }
    for name in ("cross_face", "cross_elem", "start"):
        arrays[name].start()

    barrier = pltpu.get_barrier_semaphore()
    for partner in partners:
        pl.semaphore_signal(barrier, inc=1, device_id={"mesh": partner}, device_id_type=MESH)
    for peer in peers:
        pl.semaphore_signal(barrier, inc=1, device_id={"tm": peer}, device_id_type=MESH)
    for name in list(arrays)[3:]:
        arrays[name].start()
    for load in loads:
        load.start()

    state[...] = jnp.zeros_like(state)
    resid[...] = jnp.zeros_like(resid)
    jac[...] = jnp.zeros_like(jac)
    zero_tile = jnp.zeros((8, 128), jnp.float32)
    group = lax.broadcasted_iota(jnp.int32, (8, 128), 1) // cap
    row = lax.broadcasted_iota(jnp.int32, (8, 128), 0)

    arrays["cross_face"].wait()
    arrays["cross_elem"].wait()
    cross_key = cross_face[...] * elems + cross_elem[...]
    cross_key = jnp.concatenate(
        [cross_key, jnp.full((1, lanes - slots), -1, jnp.int32)], axis=1
    )
    for face in range(6):
        rows = lax.broadcasted_iota(jnp.int32, (elems, lanes), 0) + face * elems
        hot_cross[pl.ds(face * elems, elems), :] = jnp.where(
            rows == cross_key, 1.0, 0.0
        ).astype(jnp.bfloat16)
    arrays["start"].wait()

    def prepare_inner():
        for name in ("inner_face", "inner_elem", "inner_orient", "inner_jac"):
            arrays[name].wait()
        for name in ("cross_orient", "cross_count", "cross_jac"):
            arrays[name].wait()
        inner_key = inner_face[...] * elems + inner_elem[...]
        inner_key = jnp.concatenate([inner_key[0:1], inner_key[1:2]], axis=1)
        for face in range(6):
            rows = lax.broadcasted_iota(jnp.int32, (elems, 2 * fin), 0) + face * elems
            hot_inner[pl.ds(face * elems, elems), :] = jnp.where(
                rows == inner_key, 1.0, 0.0
            ).astype(jnp.bfloat16)
        column = lax.broadcasted_iota(jnp.int32, (128, elems), 1)
        for key, table in ((inner_key, put_inner), (cross_key, put_cross)):
            for block in range(table.shape[0] // 128):
                place = slice(block * 128, (block + 1) * 128)
                spread = jnp.broadcast_to(key[:, place].astype(jnp.float32), (128, 128))
                spread = spread.T.astype(jnp.int32)
                for face in range(6):
                    table[place, face * elems : (face + 1) * elems] = jnp.where(
                        column == spread - face * elems, 1.0, 0.0
                    ).astype(jnp.bfloat16)
        for u in range(VARS):
            for v in range(VARS):
                jac[u, v : v + 1, 0:fin] = inner_jac[5 * u + v, 0:1, :]
                jac[u, v : v + 1, fin : 2 * fin] = inner_jac[5 * u + v, 1:2, :]
                jac[u, v : v + 1, 2 * fin : 2 * fin + slots] = cross_jac[5 * u + v, :, :]
        orient = inner_orient[...]
        inner_orients[...] = jnp.concatenate([orient, orient_back(orient)], axis=1)
        cross_orients[...] = jnp.concatenate(
            [cross_orient[...], jnp.zeros((1, lanes - slots), jnp.int32)], axis=1
        )
        lane = lax.broadcasted_iota(jnp.int32, (1, lanes), 1)
        live = jnp.zeros((1, lanes), jnp.int32)
        for k in range(5):
            live = jnp.where((lane >= k * cap) & (lane < k * cap + cross_count[0, k]), 1, live)
        alive[...] = live

    def send_peers(sweep):
        return [
            pltpu.make_async_remote_copy(
                src_ref=current.at[pl.ds(0, total_rows)],
                dst_ref=peer_buf.at[sweep, d],
                send_sem=peer_send_sem.at[sweep, d],
                recv_sem=peer_recv_sem.at[sweep, d],
                device_id={"tm": peers[d]},
                device_id_type=MESH,
            )
            for d in range(count_times - 1)
        ]

    def one_sweep(sweep, carry):
        first = sweep == 0

        for v in range(VARS):
            state[pl.ds(v, NODES, stride=8), :] = current[v * NODES : (v + 1) * NODES, :]
        peer_copies = send_peers(sweep)
        tiles = [
            state[8 * node : 8 * node + 8, :] * NODE_WEIGHT[node] for node in range(NODES)
        ]
        faces = jnp.concatenate(
            [
                jnp.concatenate([tiles[FACE_NODES[face][n]] for face in range(6)], axis=1)
                for n in range(9)
            ],
            axis=0,
        )
        faces = split_rows(faces)

        cross_trace = jnp.dot(faces, hot_cross[...], preferred_element_type=jnp.float32)
        cross_trace = cross_trace[0:72] + cross_trace[72:144]
        for k in range(5):
            column = (k // 4) * 128
            last = cross_trace[64:72, column : column + 128]
            last = pltpu.roll(last, -k % 4 * cap, 1) if k % 4 else last
            for h in range(2):
                packed = zero_tile
                for g in range(4):
                    n = 4 * h + g
                    piece = cross_trace[8 * n : 8 * n + 8, column : column + 128]
                    shift = (g - k % 4) * cap % 128
                    piece = pltpu.roll(piece, shift, 1) if shift else piece
                    packed = jnp.where(group == g, piece, packed)
                extra = pltpu.roll(last, 5 if h == 0 else 2, 0)
                packed = jnp.where(row >= VARS, extra, packed)
                send_buf[sweep, k, 8 * h : 8 * h + 8, :] = packed
        copies = [
            pltpu.make_async_remote_copy(
                src_ref=send_buf.at[sweep, k],
                dst_ref=recv_buf.at[sweep, MIRROR[k]],
                send_sem=send_sem.at[sweep, k],
                recv_sem=recv_sem.at[sweep, MIRROR[k]],
                device_id={"mesh": partners[k]},
                device_id_type=MESH,
            )
            for k in range(5)
        ]
        for k in (3, 2, 4, 0, 1):
            copies[k].start()

        pl.when(first)(prepare_inner)

        trace = jnp.dot(faces, hot_inner[...], preferred_element_type=jnp.float32)
        trace = trace[0:72] + trace[72:144]
        trace = [
            jnp.concatenate(
                [trace[8 * n : 8 * n + 8, fin:], trace[8 * n : 8 * n + 8, :fin]], axis=1
            )
            for n in range(9)
        ]
        trace = apply_orient(trace, inner_orients[...])
        received = apply_jacobian([jac[u, :, 0 : 2 * fin] for u in range(VARS)], trace)
        received = split_rows(jnp.concatenate(received, axis=0))
        placed = jnp.dot(received, put_inner[...], preferred_element_type=jnp.float32)
        placed = placed[0:72] + placed[72:144]
        for node, total in enumerate(node_sums(placed)):
            couple[8 * node : 8 * node + 8, :] = total

        @pl.when(first)
        def _():
            arrays["source"].wait()
            arrays["mass"].wait()

        for v in range(VARS):
            rows = slice(v * NODES, (v + 1) * NODES)
            resid[rows, :] = source[rows, :] - couple[pl.ds(v, NODES, stride=8), :]

        for copy in copies:
            copy.wait_recv()
        arrived = []
        for n in range(9):
            h, g = n // 4 % 2, n % 4
            columns = [zero_tile] * (lanes // 128)
            for k in range(5):
                piece = recv_buf[sweep, k, 8 * h : 8 * h + 8, :]
                if n == 8:
                    other = recv_buf[sweep, k, 8:16, :]
                    piece = jnp.where(row < 3, pltpu.roll(piece, 3, 0), pltpu.roll(other, 6, 0))
                shift = (k % 4 - g) * cap % 128
                piece = pltpu.roll(piece, shift, 1) if shift else piece
                columns[k // 4] = jnp.where(group == k % 4, piece, columns[k // 4])
            arrived.append(jnp.concatenate(columns, axis=1))
        arrived = apply_orient(arrived, cross_orients[...])
        received = apply_jacobian([jac[u, :, 2 * fin :] for u in range(VARS)], arrived)
        live = jnp.broadcast_to(alive[...] == 1, (8, lanes))
        received = [jnp.where(live, value, 0.0) for value in received]
        received = split_rows(jnp.concatenate(received, axis=0))
        placed = jnp.dot(received, put_cross[...], preferred_element_type=jnp.float32)
        placed = placed[0:72] + placed[72:144]
        for node, total in enumerate(node_sums(placed)):
            couple[8 * node : 8 * node + 8, :] = total

        for copy in peer_copies:
            copy.wait_recv()
        for v in range(VARS):
            rows = slice(v * NODES, (v + 1) * NODES)
            spectral = coef[1] * peer_buf[sweep, 0, rows, :]
            for d in range(1, count_times - 1):
                spectral = spectral + coef[d + 1] * peer_buf[sweep, d, rows, :]
            value = (
                resid[rows, :]
                - couple[pl.ds(v, NODES, stride=8), :]
                - mass[rows, :] * spectral
            )
            resid[rows, :] = value.astype(jnp.bfloat16).astype(jnp.float32)

        for copy in peer_copies:
            copy.wait_send()
        for copy in copies:
            copy.wait_send()

        @pl.when(first)
        def _():
            for load in loads:
                load.wait()

        top = resid[0:128, :].reshape(16, 8, 128)
        tail = resid[128:136, :]

        def row_sum(row):
            block = inv_v[row, 0:128, :].astype(jnp.float32).reshape(16, 8, 128)
            last = inv_v[row, 128:135, :].astype(jnp.float32)
            last = jnp.concatenate([last, jnp.zeros((1, 128), jnp.float32)], axis=0)
            return jnp.sum(block * top, axis=0) + last * tail

        def body(step, carry):
            for i in range(17):
                index = step * 17 + i
                partial[pl.ds(pl.multiple_of(index * 8, 8), 8), :] = row_sum(index)
            return carry

        padded = total_rows + 1
        lax.fori_loop(0, padded // 17, body, 0)
        total = partial[pl.ds(0, padded, stride=8), :]
        for i in range(1, 8):
            total = total + partial[pl.ds(i, padded, stride=8), :]
        current[...] = total

        @pl.when(sweep < SWEEPS - 1)
        def _():
            for copy in send_peers(sweep + 1):
                copy.start()

        return carry

    pl.semaphore_wait(barrier, 5 + count_times - 1)
    for copy in send_peers(0):
        copy.start()
    lax.fori_loop(0, SWEEPS, one_sweep, 0)
    out[...] = current[0:total_rows, :]


def on_device(
    inverse,
    start,
    source,
    mass,
    inner_elem,
    inner_face,
    inner_orient,
    inner_jac,
    cross_elem,
    cross_face,
    cross_orient,
    cross_count,
    cross_jac,
):
    count_times = lax.axis_size("tm")
    count_mesh = lax.axis_size("mesh")
    rows, elems = mass.shape
    fin = inner_orient.shape[0]
    slots = cross_elem.shape[1]
    lanes = -(-slots // 128) * 128
    vmem = pl.BlockSpec(memory_space=pltpu.VMEM)
    specs = [pl.BlockSpec(memory_space=pltpu.HBM)] * 13
    result = pl.pallas_call(
        functools.partial(kernel, count_times, count_mesh),
        out_shape=jax.ShapeDtypeStruct((rows, elems), jnp.float32),
        in_specs=specs,
        out_specs=vmem,
        scratch_shapes=[
            pltpu.VMEM((rows, elems), jnp.float32),
            pltpu.VMEM((rows, elems), jnp.float32),
            pltpu.VMEM((2, fin), jnp.int32),
            pltpu.VMEM((2, fin), jnp.int32),
            pltpu.VMEM((1, fin), jnp.int32),
            pltpu.VMEM((25, 2, fin), jnp.float32),
            pltpu.VMEM((1, slots), jnp.int32),
            pltpu.VMEM((1, slots), jnp.int32),
            pltpu.VMEM((1, slots), jnp.int32),
            pltpu.SMEM((1, 5), jnp.int32),
            pltpu.VMEM((25, 1, slots), jnp.float32),
            pltpu.VMEM((rows + 1, rows, elems), jnp.bfloat16),
            pltpu.VMEM((6 * elems, 2 * fin), jnp.bfloat16),
            pltpu.VMEM((6 * elems, lanes), jnp.bfloat16),
            pltpu.VMEM((2 * fin, 6 * elems), jnp.bfloat16),
            pltpu.VMEM((lanes, 6 * elems), jnp.bfloat16),
            pltpu.VMEM((8 * NODES, elems), jnp.float32),
            pltpu.VMEM((VARS, 8, 2 * fin + lanes), jnp.float32),
            pltpu.VMEM((8 * NODES, elems), jnp.float32),
            pltpu.VMEM((rows + 1, elems), jnp.float32),
            pltpu.VMEM((rows + 1, elems), jnp.float32),
            pltpu.VMEM((1, 2 * fin), jnp.int32),
            pltpu.VMEM((1, lanes), jnp.int32),
            pltpu.VMEM((1, lanes), jnp.int32),
            pltpu.VMEM((8 * (rows + 1), elems), jnp.float32),
            pltpu.VMEM((SWEEPS, 5, 16, 128), jnp.float32),
            pltpu.VMEM((SWEEPS, 5, 16, 128), jnp.float32),
            pltpu.VMEM((SWEEPS, count_times - 1, rows, elems), jnp.float32),
            pltpu.SemaphoreType.DMA((12,)),
            pltpu.SemaphoreType.DMA((5,)),
            pltpu.SemaphoreType.DMA((SWEEPS, 5)),
            pltpu.SemaphoreType.DMA((SWEEPS, 5)),
            pltpu.SemaphoreType.DMA((SWEEPS, count_times - 1)),
            pltpu.SemaphoreType.DMA((SWEEPS, count_times - 1)),
        ],
        compiler_params=pltpu.CompilerParams(
            collective_id=0, has_side_effects=True, vmem_limit_bytes=32 * 1024 * 1024
        ),
    )(
        *[
            pltpu.with_memory_space_constraint(operand, pltpu.HBM)
            for operand in (
                inverse[0],
                jnp.transpose(start, (1, 0, 2)),
                jnp.transpose(source, (1, 0, 2)),
                mass,
                inner_elem,
                inner_face,
                inner_orient.reshape(1, fin),
                jnp.transpose(inner_jac[0], (1, 0, 2)),
                cross_elem,
                cross_face,
                cross_orient,
                cross_count,
                cross_jac[0],
            )
        ]
    )
    return result[None]


def solution(mesh):
    in_specs = (
        P("tm", None, None, "mesh"),
        P("tm", None, "mesh"),
        P("tm", None, "mesh"),
        P(None, "mesh"),
        P(None, "mesh"),
        P(None, "mesh"),
        P("mesh"),
        P("tm", None, None, "mesh"),
        P("mesh", None),
        P("mesh", None),
        P("mesh", None),
        P("mesh", None),
        P("tm", None, "mesh", None),
    )
    out_specs = P("tm", None, "mesh")
    return jax.shard_map(
        on_device, mesh=mesh, in_specs=in_specs, out_specs=out_specs, check_vma=False
    )
```

```python
import functools
import math

import jax
import jax.numpy as jnp
import numpy as np
from jax import lax
from jax.experimental import pallas as pl
from jax.experimental.pallas import tpu as pltpu
from jax.sharding import PartitionSpec as P

SWEEPS = 2
VARS = 5
NODES = 27
MIRROR = (1, 0, 4, 3, 2)
LINE_WEIGHTS = (1.0 / 3.0, 4.0 / 3.0, 1.0 / 3.0)
MESH = pl.DeviceIdType.MESH


def face_table():
    nodes = [[0] * 9 for _ in range(6)]
    weight = [1.0] * NODES
    for face in range(6):
        normal = face // 2
        tangent = [axis for axis in range(3) if axis != normal]
        for j in range(3):
            for i in range(3):
                coords = [0, 0, 0]
                coords[normal] = 2 * (face % 2)
                coords[tangent[0]] = i
                coords[tangent[1]] = j
                node = 9 * coords[2] + 3 * coords[1] + coords[0]
                nodes[face][3 * j + i] = node
                weight[node] = float(np.float32(LINE_WEIGHTS[i] * LINE_WEIGHTS[j]))
    return nodes, weight


FACE_NODES, NODE_WEIGHT = face_table()


def coef_table(count):
    table = [0.0] * count
    for k in range(1, count):
        parity = (-1.0) ** k
        phase = math.pi * k / count
        table[k] = 0.3 * parity * math.cos(phase) / math.sin(phase) + 1.2 * parity / count
    return [float(np.float32(c)) for c in table]


def orient_back(orient):
    swapped = 4 + 2 * (orient & 1) + ((orient >> 1) & 1)
    return jnp.where(orient >= 4, swapped, orient)


def apply_orient(trace, orient):
    shape = trace[0].shape
    flip_i = jnp.broadcast_to((orient & 1) == 1, shape)
    flip_j = jnp.broadcast_to((orient & 2) == 2, shape)
    swap = jnp.broadcast_to(orient >= 4, shape)
    step = [
        trace[3 * j + i] if i == 1 else jnp.where(flip_i, trace[3 * j + 2 - i], trace[3 * j + i])
        for j in range(3)
        for i in range(3)
    ]
    step = [
        step[3 * j + i] if j == 1 else jnp.where(flip_j, step[3 * (2 - j) + i], step[3 * j + i])
        for j in range(3)
        for i in range(3)
    ]
    return [
        step[3 * j + i] if i == j else jnp.where(swap, step[3 * i + j], step[3 * j + i])
        for j in range(3)
        for i in range(3)
    ]


def apply_jacobian(jac, trace):
    received = []
    for value in trace:
        total = jac[0] * value[0:1, :]
        for u in range(1, VARS):
            total = total + jac[u] * value[u : u + 1, :]
        received.append(total)
    return received


def node_sums(placed):
    totals = [None] * NODES
    for face in range(6):
        for n in range(9):
            node = FACE_NODES[face][n]
            piece = placed[8 * n : 8 * n + 8, face * 128 : (face + 1) * 128]
            totals[node] = piece if totals[node] is None else totals[node] + piece
    zero = jnp.zeros((8, 128), jnp.float32)
    return [zero if total is None else total for total in totals]


def kernel(
    count_times,
    count_mesh,
    inverse,
    start_h,
    source_h,
    mass_h,
    inner_elem_h,
    inner_face_h,
    inner_orient_h,
    inner_jac_h,
    cross_elem_h,
    cross_face_h,
    cross_orient_h,
    cross_count_h,
    cross_jac_h,
    out,
    source,
    mass,
    inner_elem,
    inner_face,
    inner_orient,
    inner_jac,
    cross_elem,
    cross_face,
    cross_orient,
    cross_count,
    cross_jac,
    inv_v,
    hot_inner,
    hot_cross,
    state,
    jac,
    couple,
    resid,
    current,
    inner_orients,
    cross_orients,
    alive,
    partial,
    send_buf,
    recv_buf,
    peer_buf,
    load_sem,
    inv_sem,
    send_sem,
    recv_sem,
    peer_send_sem,
    peer_recv_sem,
):
    total_rows, elems = mass.shape
    fin = inner_orient.shape[1]
    slots = cross_orient.shape[1]
    cap = slots // 5
    lanes = hot_cross.shape[1]
    chunk = total_rows // 5
    me = lax.axis_index("mesh")
    mine = lax.axis_index("tm")
    offsets = [1, count_mesh - 1, count_mesh // 2 - 1, count_mesh // 2, count_mesh // 2 + 1]
    partners = [lax.rem(me + off, count_mesh) for off in offsets]
    peers = [lax.rem(mine - d + count_times, count_times) for d in range(1, count_times)]
    coef = coef_table(count_times)

    loads = [
        pltpu.make_async_copy(
            inverse.at[pl.ds(c * chunk, chunk)], inv_v.at[pl.ds(c * chunk, chunk)], inv_sem.at[c]
        )
        for c in range(5)
    ]
    pairs = {
        "cross_face": (cross_face_h, cross_face),
        "cross_elem": (cross_elem_h, cross_elem),
        "start": (start_h.at[:, 0], current.at[pl.ds(0, total_rows)]),
        "inner_face": (inner_face_h, inner_face),
        "inner_elem": (inner_elem_h, inner_elem),
        "inner_orient": (inner_orient_h, inner_orient),
        "inner_jac": (inner_jac_h, inner_jac),
        "cross_orient": (cross_orient_h, cross_orient),
        "cross_count": (cross_count_h, cross_count),
        "cross_jac": (cross_jac_h, cross_jac),
        "source": (source_h.at[:, 0], source),
        "mass": (mass_h, mass),
    }
    arrays = {
        name: pltpu.make_async_copy(src, dst, load_sem.at[index])
        for index, (name, (src, dst)) in enumerate(pairs.items())
    }
    for name in ("cross_face", "cross_elem", "start"):
        arrays[name].start()

    barrier = pltpu.get_barrier_semaphore()
    for partner in partners:
        pl.semaphore_signal(barrier, inc=1, device_id={"mesh": partner}, device_id_type=MESH)
    for peer in peers:
        pl.semaphore_signal(barrier, inc=1, device_id={"tm": peer}, device_id_type=MESH)
    for name in list(arrays)[3:]:
        arrays[name].start()
    for load in loads:
        load.start()

    state[...] = jnp.zeros_like(state)
    resid[...] = jnp.zeros_like(resid)
    jac[...] = jnp.zeros_like(jac)
    zero_tile = jnp.zeros((8, 128), jnp.float32)
    group = lax.broadcasted_iota(jnp.int32, (8, 128), 1) // cap
    row = lax.broadcasted_iota(jnp.int32, (8, 128), 0)

    arrays["cross_face"].wait()
    arrays["cross_elem"].wait()
    cross_key = cross_face[...] * elems + cross_elem[...]
    cross_key = jnp.concatenate(
        [cross_key, jnp.full((1, lanes - slots), -1, jnp.int32)], axis=1
    )
    for face in range(6):
        rows = lax.broadcasted_iota(jnp.int32, (elems, lanes), 0) + face * elems
        hot_cross[pl.ds(face * elems, elems), :] = jnp.where(
            rows == cross_key, 1.0, 0.0
        ).astype(jnp.bfloat16)
    arrays["start"].wait()

    def prepare_inner():
        for name in ("inner_face", "inner_elem", "inner_orient", "inner_jac"):
            arrays[name].wait()
        for name in ("cross_orient", "cross_count", "cross_jac"):
            arrays[name].wait()
        inner_key = inner_face[...] * elems + inner_elem[...]
        inner_key = jnp.concatenate([inner_key[0:1], inner_key[1:2]], axis=1)
        for face in range(6):
            rows = lax.broadcasted_iota(jnp.int32, (elems, 2 * fin), 0) + face * elems
            hot_inner[pl.ds(face * elems, elems), :] = jnp.where(
                rows == inner_key, 1.0, 0.0
            ).astype(jnp.bfloat16)
        for u in range(VARS):
            for v in range(VARS):
                jac[u, v : v + 1, 0:fin] = inner_jac[5 * u + v, 0:1, :]
                jac[u, v : v + 1, fin : 2 * fin] = inner_jac[5 * u + v, 1:2, :]
                jac[u, v : v + 1, 2 * fin : 2 * fin + slots] = cross_jac[5 * u + v, :, :]
        orient = inner_orient[...]
        inner_orients[...] = jnp.concatenate([orient, orient_back(orient)], axis=1)
        cross_orients[...] = jnp.concatenate(
            [cross_orient[...], jnp.zeros((1, lanes - slots), jnp.int32)], axis=1
        )
        lane = lax.broadcasted_iota(jnp.int32, (1, lanes), 1)
        live = jnp.zeros((1, lanes), jnp.int32)
        for k in range(5):
            live = jnp.where((lane >= k * cap) & (lane < k * cap + cross_count[0, k]), 1, live)
        alive[...] = live

    def send_peers(sweep):
        return [
            pltpu.make_async_remote_copy(
                src_ref=current.at[pl.ds(0, total_rows)],
                dst_ref=peer_buf.at[sweep, d],
                send_sem=peer_send_sem.at[sweep, d],
                recv_sem=peer_recv_sem.at[sweep, d],
                device_id={"tm": peers[d]},
                device_id_type=MESH,
            )
            for d in range(count_times - 1)
        ]

    def one_sweep(sweep, carry):
        first = sweep == 0

        for v in range(VARS):
            state[pl.ds(v, NODES, stride=8), :] = current[v * NODES : (v + 1) * NODES, :]
        peer_copies = send_peers(sweep)
        tiles = [
            state[8 * node : 8 * node + 8, :] * NODE_WEIGHT[node] for node in range(NODES)
        ]
        faces = jnp.concatenate(
            [
                jnp.concatenate([tiles[FACE_NODES[face][n]] for face in range(6)], axis=1)
                for n in range(9)
            ],
            axis=0,
        )
        faces = faces.astype(jnp.bfloat16)

        cross_trace = jnp.dot(faces, hot_cross[...], preferred_element_type=jnp.float32)
        for k in range(5):
            column = (k // 4) * 128
            last = cross_trace[64:72, column : column + 128]
            last = pltpu.roll(last, -k % 4 * cap, 1) if k % 4 else last
            for h in range(2):
                packed = zero_tile
                for g in range(4):
                    n = 4 * h + g
                    piece = cross_trace[8 * n : 8 * n + 8, column : column + 128]
                    shift = (g - k % 4) * cap % 128
                    piece = pltpu.roll(piece, shift, 1) if shift else piece
                    packed = jnp.where(group == g, piece, packed)
                extra = pltpu.roll(last, 5 if h == 0 else 2, 0)
                packed = jnp.where(row >= VARS, extra, packed)
                send_buf[sweep, k, 8 * h : 8 * h + 8, :] = packed

        @pl.when(first)
        def _():
            pl.semaphore_wait(barrier, 5 + count_times - 1)

        copies = [
            pltpu.make_async_remote_copy(
                src_ref=send_buf.at[sweep, k],
                dst_ref=recv_buf.at[sweep, MIRROR[k]],
                send_sem=send_sem.at[sweep, k],
                recv_sem=recv_sem.at[sweep, MIRROR[k]],
                device_id={"mesh": partners[k]},
                device_id_type=MESH,
            )
            for k in range(5)
        ]
        for k in (3, 2, 4, 0, 1):
            copies[k].start()

        @pl.when(first)
        def _():
            for copy in peer_copies:
                copy.start()
            prepare_inner()

        trace = jnp.dot(faces, hot_inner[...], preferred_element_type=jnp.float32)
        trace = [
            jnp.concatenate(
                [trace[8 * n : 8 * n + 8, fin:], trace[8 * n : 8 * n + 8, :fin]], axis=1
            )
            for n in range(9)
        ]
        trace = apply_orient(trace, inner_orients[...])
        received = apply_jacobian([jac[u, :, 0 : 2 * fin] for u in range(VARS)], trace)
        received = jnp.concatenate(received, axis=0).astype(jnp.bfloat16)
        placed = lax.dot_general(
            received,
            hot_inner[...],
            (((1,), (1,)), ((), ())),
            preferred_element_type=jnp.float32,
        )
        for node, total in enumerate(node_sums(placed)):
            couple[8 * node : 8 * node + 8, :] = total

        @pl.when(first)
        def _():
            arrays["source"].wait()
            arrays["mass"].wait()

        for v in range(VARS):
            rows = slice(v * NODES, (v + 1) * NODES)
            resid[rows, :] = source[rows, :] - couple[pl.ds(v, NODES, stride=8), :]

        for copy in copies:
            copy.wait_recv()
        arrived = []
        for n in range(9):
            h, g = n // 4 % 2, n % 4
            columns = [zero_tile] * (lanes // 128)
            for k in range(5):
                piece = recv_buf[sweep, k, 8 * h : 8 * h + 8, :]
                if n == 8:
                    other = recv_buf[sweep, k, 8:16, :]
                    piece = jnp.where(row < 3, pltpu.roll(piece, 3, 0), pltpu.roll(other, 6, 0))
                shift = (k % 4 - g) * cap % 128
                piece = pltpu.roll(piece, shift, 1) if shift else piece
                columns[k // 4] = jnp.where(group == k % 4, piece, columns[k // 4])
            arrived.append(jnp.concatenate(columns, axis=1))
        arrived = apply_orient(arrived, cross_orients[...])
        received = apply_jacobian([jac[u, :, 2 * fin :] for u in range(VARS)], arrived)
        live = jnp.broadcast_to(alive[...] == 1, (8, lanes))
        received = [jnp.where(live, value, 0.0) for value in received]
        received = jnp.concatenate(received, axis=0).astype(jnp.bfloat16)
        placed = lax.dot_general(
            received,
            hot_cross[...],
            (((1,), (1,)), ((), ())),
            preferred_element_type=jnp.float32,
        )
        for node, total in enumerate(node_sums(placed)):
            couple[8 * node : 8 * node + 8, :] = total

        for copy in peer_copies:
            copy.wait_recv()
        for v in range(VARS):
            rows = slice(v * NODES, (v + 1) * NODES)
            spectral = coef[1] * peer_buf[sweep, 0, rows, :]
            for d in range(1, count_times - 1):
                spectral = spectral + coef[d + 1] * peer_buf[sweep, d, rows, :]
            value = (
                resid[rows, :]
                - couple[pl.ds(v, NODES, stride=8), :]
                - mass[rows, :] * spectral
            )
            resid[rows, :] = value.astype(jnp.bfloat16).astype(jnp.float32)

        for copy in peer_copies:
            copy.wait_send()
        for copy in copies:
            copy.wait_send()

        @pl.when(first)
        def _():
            for load in loads:
                load.wait()

        top = resid[0:128, :].reshape(16, 8, 128)
        tail = resid[128:136, :]

        def row_sum(row):
            block = inv_v[row, 0:128, :].astype(jnp.float32).reshape(16, 8, 128)
            last = inv_v[row, 128:135, :].astype(jnp.float32)
            last = jnp.concatenate([last, jnp.zeros((1, 128), jnp.float32)], axis=0)
            return jnp.sum(block * top, axis=0) + last * tail

        def body(step, carry):
            for i in range(17):
                index = step * 17 + i
                partial[pl.ds(pl.multiple_of(index * 8, 8), 8), :] = row_sum(index)
            return carry

        padded = total_rows + 1
        lax.fori_loop(0, padded // 17, body, 0)
        total = partial[pl.ds(0, padded, stride=8), :]
        for i in range(1, 8):
            total = total + partial[pl.ds(i, padded, stride=8), :]
        current[...] = total

        @pl.when(sweep < SWEEPS - 1)
        def _():
            for copy in send_peers(sweep + 1):
                copy.start()

        return carry

    lax.fori_loop(0, SWEEPS, one_sweep, 0)
    out[...] = current[0:total_rows, :]


def on_device(
    inverse,
    start,
    source,
    mass,
    inner_elem,
    inner_face,
    inner_orient,
    inner_jac,
    cross_elem,
    cross_face,
    cross_orient,
    cross_count,
    cross_jac,
):
    count_times = lax.axis_size("tm")
    count_mesh = lax.axis_size("mesh")
    rows, elems = mass.shape
    fin = inner_orient.shape[0]
    slots = cross_elem.shape[1]
    lanes = -(-slots // 128) * 128
    vmem = pl.BlockSpec(memory_space=pltpu.VMEM)
    specs = [pl.BlockSpec(memory_space=pltpu.HBM)] * 13
    result = pl.pallas_call(
        functools.partial(kernel, count_times, count_mesh),
        out_shape=jax.ShapeDtypeStruct((rows, elems), jnp.float32),
        in_specs=specs,
        out_specs=vmem,
        scratch_shapes=[
            pltpu.VMEM((rows, elems), jnp.float32),
            pltpu.VMEM((rows, elems), jnp.float32),
            pltpu.VMEM((2, fin), jnp.int32),
            pltpu.VMEM((2, fin), jnp.int32),
            pltpu.VMEM((1, fin), jnp.int32),
            pltpu.VMEM((25, 2, fin), jnp.float32),
            pltpu.VMEM((1, slots), jnp.int32),
            pltpu.VMEM((1, slots), jnp.int32),
            pltpu.VMEM((1, slots), jnp.int32),
            pltpu.SMEM((1, 5), jnp.int32),
            pltpu.VMEM((25, 1, slots), jnp.float32),
            pltpu.VMEM((rows + 1, rows, elems), jnp.bfloat16),
            pltpu.VMEM((6 * elems, 2 * fin), jnp.bfloat16),
            pltpu.VMEM((6 * elems, lanes), jnp.bfloat16),
            pltpu.VMEM((8 * NODES, elems), jnp.float32),
            pltpu.VMEM((VARS, 8, 2 * fin + lanes), jnp.float32),
            pltpu.VMEM((8 * NODES, elems), jnp.float32),
            pltpu.VMEM((rows + 1, elems), jnp.float32),
            pltpu.VMEM((rows + 1, elems), jnp.float32),
            pltpu.VMEM((1, 2 * fin), jnp.int32),
            pltpu.VMEM((1, lanes), jnp.int32),
            pltpu.VMEM((1, lanes), jnp.int32),
            pltpu.VMEM((8 * (rows + 1), elems), jnp.float32),
            pltpu.VMEM((SWEEPS, 5, 16, 128), jnp.float32),
            pltpu.VMEM((SWEEPS, 5, 16, 128), jnp.float32),
            pltpu.VMEM((SWEEPS, count_times - 1, rows, elems), jnp.float32),
            pltpu.SemaphoreType.DMA((12,)),
            pltpu.SemaphoreType.DMA((5,)),
            pltpu.SemaphoreType.DMA((SWEEPS, 5)),
            pltpu.SemaphoreType.DMA((SWEEPS, 5)),
            pltpu.SemaphoreType.DMA((SWEEPS, count_times - 1)),
            pltpu.SemaphoreType.DMA((SWEEPS, count_times - 1)),
        ],
        compiler_params=pltpu.CompilerParams(
            collective_id=0, has_side_effects=True, vmem_limit_bytes=32 * 1024 * 1024
        ),
    )(
        *[
            pltpu.with_memory_space_constraint(operand, pltpu.HBM)
            for operand in (
                inverse[0],
                jnp.transpose(start, (1, 0, 2)),
                jnp.transpose(source, (1, 0, 2)),
                mass,
                inner_elem,
                inner_face,
                inner_orient.reshape(1, fin),
                jnp.transpose(inner_jac[0], (1, 0, 2)),
                cross_elem,
                cross_face,
                cross_orient,
                cross_count,
                cross_jac[0],
            )
        ]
    )
    return result[None]


def solution(mesh):
    in_specs = (
        P("tm", None, None, "mesh"),
        P("tm", None, "mesh"),
        P("tm", None, "mesh"),
        P(None, "mesh"),
        P(None, "mesh"),
        P(None, "mesh"),
        P("mesh"),
        P("tm", None, None, "mesh"),
        P("mesh", None),
        P("mesh", None),
        P("mesh", None),
        P("mesh", None),
        P("tm", None, "mesh", None),
    )
    out_specs = P("tm", None, "mesh")
    return jax.shard_map(
        on_device, mesh=mesh, in_specs=in_specs, out_specs=out_specs, check_vma=False
    )
```
